32 devices in a mesh: tok: 8 (over z, core), ten: 4 (over y, x).
Axes of the slice: x: 2, y: 2, z: 4, core: 2. Of those that a mesh axis runs over, the one named last changes fastest.
Arguments:
- counts: int32 [1024, 128256], P('ten', 'tok'), may hold values from 0 to 31
- u_factor: float32 [64, 1024], P('tok', 'ten'), may hold values from -2.5 to 2.5
- u_accum: float32 [64, 1024], P('tok', 'ten'), may hold values from 8016 to 513024
- v_factor: float32 [64, 128256], P('ten', 'tok'), may hold values from -2.5 to 2.5
- v_accum: float32 [64, 128256], P('ten', 'tok'), may hold values from 64 to 4096
Outputs:
- u_next: float32 [64, 1024], P('tok', 'ten')
- u_accum_next: float32 [64, 1024], P('tok', 'ten')
- v_next: float32 [64, 128256], P('ten', 'tok')
- v_accum_next: float32 [64, 128256], P('ten', 'tok')
The draws below stay inside these ranges and needn't reach their ends.
All inputs are finite; a program needn't handle non-finite values.
Results may differ from the reference program's by a relative error of at most 0.0076.
Values may be sent and summed in bfloat16 or wider, within the bound.
No kernel may reach another device: no remote copies, remote signals or barrier semaphores. Data moves between devices by JAX's collectives and lax.ppermute only.
A program may use at most 64 MiB of HBM per device.

```python
import math
import jax
import jax.numpy as jnp
import numpy as np
from jax import lax

RANK = 64
VOCAB = 128256
TEN_DEV = 256
TENANTS = 1024


def place_ends(values, stream_key, smallest, high):
    shape = values.shape
    index_at = [jax.random.randint(jax.random.fold_in(stream_key, axis), (), 0, shape[axis]) for axis in range(len(shape))]
    values = values.at[tuple(index_at)].set(smallest)
    longest = shape.index(max(shape))
    index_at[longest] = (index_at[longest] + 1) % shape[longest]
    return values.at[tuple(index_at)].set(high)


def strengthened(drawn, rng, source, target, shards_of, factor):
    owner, partner = [(jnp.arange(drawn.shape[dim]) // (drawn.shape[dim] // shards_of)).reshape([-1 if axis == dim else 1 for axis in range(drawn.ndim)]) for dim in (source, target)]
    chosen = jax.random.permutation(rng, shards_of)[partner]
    strong = (owner == chosen) | (owner == (partner + shards_of // 2) % shards_of)
    return jnp.where(strong, factor * drawn, drawn)


def steps_of(stream_key, dims, shards, smallest, top_value):
    loudness, own = 1.0, jax.random.fold_in(stream_key, 6)
    for position, shards_of in shards:
        draws = jnp.exp(jax.random.uniform(jax.random.fold_in(own, position), (shards_of,), jnp.float32, smallest / len(shards), top_value / len(shards)))
        loudness = loudness * jnp.repeat(draws, dims[position] // shards_of).reshape([-1 if axis == position else 1 for axis in range(len(dims))])
    return loudness


def cumulative_ranks(count, slope):
    weights = [(1 << 20) // math.isqrt(rank ** slope) + 1 for rank in range(1, count + 1)]
    deviation = 1 + sum(weights) // (1 << 30)
    return np.cumsum(np.array([max(1, weight // deviation) for weight in weights]))


def ranked(stream_key, shape, number_of, skew):
    grid = cumulative_ranks(number_of, skew)
    lot = jax.random.randint(jax.random.fold_in(stream_key, 1), shape, 0, int(grid[number_of - 1]))
    grade = jnp.searchsorted(jnp.asarray(grid, jnp.int32), lot, side="right")
    return jax.random.permutation(jax.random.fold_in(stream_key, 2), number_of)[grade].astype(jnp.int32)


def noise_with(key, shape, width, bound, split, heavy, held_as=jnp.bfloat16):
    result = width * jax.random.normal(key, shape, jnp.float32)
    if split:
        result = result * steps_of(key, shape, split, -0.22, 0.18)
    return jnp.clip(strengthened(result, jax.random.fold_in(key, 3), *heavy), -bound, bound).astype(held_as)


def setup_inputs(seed: int = 0) -> dict:
    key_list = jax.random.split(jax.random.key(seed), 6)
    counts = place_ends(ranked(key_list[0], (TENANTS, VOCAB), 32, 2), jax.random.fold_in(key_list[0], 3), 0, 31).astype(jnp.int32)
    u_factor = noise_with(key_list[1], (RANK, TENANTS), 0.35, 2.5, ((0, 8), (1, 4)), (1, 0, 8, 2.0), jnp.float32)
    u_accum = jnp.clip(jnp.exp(math.log(513024.0) - 4.158883 * jax.random.uniform(key_list[2], (RANK, TENANTS), jnp.float32) ** steps_of(key_list[2], (RANK, TENANTS), ((0, 8), (1, 4)), -0.2, 0.2)), 8016.0, 513024.0)
    v_factor = noise_with(key_list[3], (RANK, VOCAB), 0.35, 2.5, ((0, 4), (1, 8)), (1, 0, 8, 2.0), jnp.float32)
    v_accum = jnp.clip(jnp.exp(math.log(4096.0) - 4.158883 * jax.random.uniform(key_list[4], (RANK, VOCAB), jnp.float32) ** steps_of(key_list[4], (RANK, VOCAB), ((0, 4), (1, 8)), -0.2, 0.2)), 64.0, 4096.0)
    return dict(counts=counts, u_factor=u_factor, u_accum=u_accum, v_factor=v_factor, v_accum=v_accum)


weight_scale = 0.5
step_rate = 0.3

def residual(low_block, v_low, count_block):
    logits = jnp.dot(low_block.T, v_low, preferred_element_type=jnp.float32)
    weighted = weight_scale * count_block.astype(jnp.float32)
    return (weighted - (1.0 + weighted) * jax.nn.sigmoid(logits)).astype(jnp.bfloat16)

def reference(counts, u_factor, u_accum, v_factor, v_accum):
    blocks = TENANTS // TEN_DEV
    u_low = u_factor.astype(jnp.bfloat16)
    v_low = v_factor.astype(jnp.bfloat16)
    count_blocks = counts.reshape(blocks, TEN_DEV, VOCAB)
    u_blocks = u_low.reshape(RANK, blocks, TEN_DEV).transpose(1, 0, 2)

    def grad_block(pair):
        low_block, count_block = pair
        resid = residual(low_block, v_low, count_block)
        return jnp.dot(v_low, resid.T, preferred_element_type=jnp.float32)
    grads = lax.map(grad_block, (u_blocks, count_blocks))
    grad_u = grads.transpose(1, 0, 2).reshape(RANK, TENANTS)
    u_accum_next = u_accum + grad_u * grad_u
    u_next = u_factor + step_rate * grad_u / jnp.sqrt(u_accum_next)
    fresh_blocks = u_next.astype(jnp.bfloat16).reshape(RANK, blocks, TEN_DEV).transpose(1, 0, 2)

    def add_block(total, pair):
        low_block, count_block = pair
        resid = residual(low_block, v_low, count_block)
        return (total + jnp.dot(low_block, resid, preferred_element_type=jnp.float32), None)
    grad_v, _ = lax.scan(add_block, jnp.zeros((RANK, VOCAB), jnp.float32), (fresh_blocks, count_blocks))
    v_accum_next = v_accum + grad_v * grad_v
    v_next = v_factor + step_rate * grad_v / jnp.sqrt(v_accum_next)
    return (u_next, u_accum_next, v_next, v_accum_next)
```

```python
import jax
import jax.numpy as jnp
from jax import lax
from jax.experimental import pallas as pl
from jax.experimental.pallas import tpu as pltpu
from jax.sharding import PartitionSpec as P

weight_scale = 0.5
step_rate = 0.3
LANES = 128
CHUNK = 6144
INNER = 1024
VMEM_LIMIT = 30 * 2**20

whole = pl.BlockSpec(memory_space=pltpu.VMEM)
scalars = pl.BlockSpec(memory_space=pltpu.SMEM)


def residual(low_tile, v_tile, counts):
    logits = lax.dot_general(
        low_tile, v_tile, (((0,), (0,)), ((), ())), preferred_element_type=jnp.float32
    )
    weighted = weight_scale * counts.astype(jnp.float32)
    return (weighted - (1.0 + weighted) * jax.nn.sigmoid(logits)).astype(jnp.bfloat16)


def gather_tenant(low_rows):
    return lax.all_gather(low_rows, "tok", axis=0, tiled=True)


def shards_any(counts, u_factor, u_accum, v_factor, v_accum):
    v_tile = lax.all_gather(v_factor.astype(jnp.bfloat16), "ten", axis=0, tiled=True)
    u_tile = gather_tenant(u_factor.astype(jnp.bfloat16))
    resid = residual(u_tile, v_tile, counts)
    grad_u = lax.psum_scatter(
        lax.dot_general(
            v_tile, resid, (((1,), (1,)), ((), ())), preferred_element_type=jnp.float32
        ),
        "tok",
        scatter_dimension=0,
        tiled=True,
    )
    u_accum_next = u_accum + grad_u * grad_u
    u_next = u_factor + step_rate * grad_u / jnp.sqrt(u_accum_next)
    u_fresh = gather_tenant(u_next.astype(jnp.bfloat16))
    resid_fresh = residual(u_fresh, v_tile, counts)
    grad_v = lax.psum_scatter(
        jnp.dot(u_fresh, resid_fresh, preferred_element_type=jnp.float32),
        "ten",
        scatter_dimension=0,
        tiled=True,
    )
    v_accum_next = v_accum + grad_v * grad_v
    v_next = v_factor + step_rate * grad_v / jnp.sqrt(v_accum_next)
    return (u_next, u_accum_next, v_next, v_accum_next)


def swap(a, axis, bit, size):
    return lax.ppermute(a, axis, [(i, i ^ bit) for i in range(size)])


def call(kernel, out_shape, operands, in_specs, flops=0, moved=0, **options):
    return pl.pallas_call(
        kernel,
        out_shape=out_shape,
        in_specs=in_specs,
        compiler_params=pltpu.CompilerParams(vmem_limit_bytes=VMEM_LIMIT),
        cost_estimate=pl.CostEstimate(
            flops=flops, bytes_accessed=moved, transcendentals=0
        ),
        **options,
    )(*operands)


def order_tenant(place, gathered):
    def kernel(place_ref, all_ref, factor_ref, accum_ref, half_ref):
        for j in range(4):
            for h in range(2):
                source = (2 * (place_ref[1] ^ j) + h) ^ place_ref[0]
                rows = pl.ds(16 * j + 8 * h, 8)
                factor_ref[rows, :] = all_ref[source, :8, :]
                accum_ref[rows, :] = all_ref[source, 8:, :]
        half_ref[...] = (factor_ref[...].astype(jnp.bfloat16).astype(jnp.float32) * 0.5).astype(
            jnp.bfloat16
        )

    width = gathered.shape[2]
    return call(
        kernel,
        (
            jax.ShapeDtypeStruct((64, width), jnp.float32),
            jax.ShapeDtypeStruct((64, width), jnp.float32),
            jax.ShapeDtypeStruct((64, width), jnp.bfloat16),
        ),
        (place, gathered),
        [scalars, whole],
        out_specs=(whole, whole, whole),
    )


def update_tenant(place, mine, other, factor, accum):
    def kernel(place_ref, a_ref, b_ref, factor_ref, accum_ref, low_ref, half_ref, next_ref, sums_ref, full_ref, tot_ref):
        grad = a_ref[...] + b_ref[...]
        total = accum_ref[...] + grad * grad
        fresh = factor_ref[...] + step_rate * grad * lax.rsqrt(total)
        full_ref[...] = fresh
        tot_ref[...] = total
        low = fresh.astype(jnp.bfloat16)
        low_ref[...] = low
        half_ref[...] = (low.astype(jnp.float32) * 0.5).astype(jnp.bfloat16)
        row = ((place_ref[0] // 2) ^ place_ref[1]) * 16 + (place_ref[0] % 2) * 8
        rows = pl.ds(pl.multiple_of(row, 8), 8)
        next_ref[...] = full_ref[rows, :]
        sums_ref[...] = tot_ref[rows, :]

    width = mine.shape[1]
    return call(
        kernel,
        (
            jax.ShapeDtypeStruct((64, width), jnp.bfloat16),
            jax.ShapeDtypeStruct((64, width), jnp.bfloat16),
            jax.ShapeDtypeStruct((8, width), jnp.float32),
            jax.ShapeDtypeStruct((8, width), jnp.float32),
        ),
        (place, mine, other, factor, accum),
        [scalars, whole, whole, whole, whole],
        out_specs=(whole,) * 4,
        scratch_shapes=[pltpu.VMEM((64, width), jnp.float32)] * 2,
    )


def pieces(start, size, tokens):
    found = []
    half = size // 2
    for side in range(2):
        for at in range(side * half, (side + 1) * half, INNER):
            length = min(INNER, (side + 1) * half - at)
            valid = max(0, min(length, tokens - start - at))
            found.append((side, at, length, valid))
    return found


def fresh_residual(half_low, v, counts_ref, row, valid):
    logits = lax.dot_general(
        v, half_low, (((0,), (0,)), ((), ())), preferred_element_type=jnp.float32
    )[:valid]
    bend = jnp.tanh(logits)
    lift = counts_ref[row : row + valid, :].astype(jnp.float32) * 0.25 + 0.5
    resid = (lift - lift * bend - 1.0).astype(jnp.bfloat16)
    if valid < v.shape[1]:
        pad = jnp.zeros((v.shape[1] - valid, resid.shape[1]), jnp.bfloat16)
        resid = jnp.concatenate([resid, pad], axis=0)
    return resid


def tenant_grad(start, size, half_low, blocks, counts, total):
    tokens, width = counts.shape

    def kernel(half_ref, own, x, y, d0, d1, counts_ref, *rest):
        out_ref = rest[-1]
        half = size // 2
        grad = rest[0][...] if len(rest) == 2 else jnp.zeros(out_ref.shape, jnp.float32)
        for side, at, length, valid in pieces(start, size, tokens):
            if valid == 0:
                continue
            diag = (d0, d1)[side][:, at - side * half : at - side * half + length]
            v = jnp.concatenate([r[:, at : at + length] for r in (own, x, y)] + [diag], axis=0)
            resid = fresh_residual(half_ref[...], v, counts_ref, start + at, valid)
            grad += jnp.dot(v, resid, preferred_element_type=jnp.float32)
        out_ref[...] = grad

    extra = () if total is None else (total,)
    return call(
        kernel,
        jax.ShapeDtypeStruct((64, width), jnp.float32),
        (half_low, *blocks, counts) + extra,
        [whole] * (7 + len(extra)),
        flops=4 * 64 * width * size,
        moved=4 * width * size,
        out_specs=whole,
    )


def token_grad(start, size, low, half_low, blocks, counts):
    tokens, width = counts.shape
    half = size // 2

    def kernel(low_ref, half_ref, own, x, y, d0, d1, counts_ref, mine, sx, kx, sy, ky):
        for side, at, length, valid in pieces(start, size, tokens):
            lo = at - side * half
            diag = (d0, d1)[side][:, lo : lo + length]
            v = jnp.concatenate([r[:, at : at + length] for r in (own, x, y)] + [diag], axis=0)
            if valid == 0:
                grad = jnp.zeros((64, length), jnp.float32)
            else:
                resid = fresh_residual(half_ref[...], v, counts_ref, start + at, valid)
                grad = lax.dot_general(
                    low_ref[...], resid, (((1,), (1,)), ((), ())), preferred_element_type=jnp.float32
                )
            mine[:, at : at + length] = grad[:16]
            send, keep = ((sx, kx), (sy, ky))[side]
            first, kept = ((16, 32), (32, 16))[side]
            here = slice(lo, lo + length)
            send[:16, here] = grad[first : first + 16].astype(jnp.bfloat16)
            send[16:, here] = grad[48:].astype(jnp.bfloat16)
            keep[:, here] = grad[kept : kept + 16]

    return call(
        kernel,
        (
            jax.ShapeDtypeStruct((16, size), jnp.float32),
            jax.ShapeDtypeStruct((32, half), jnp.bfloat16),
            jax.ShapeDtypeStruct((16, half), jnp.float32),
            jax.ShapeDtypeStruct((32, half), jnp.bfloat16),
            jax.ShapeDtypeStruct((16, half), jnp.float32),
        ),
        (low, half_low, *blocks, counts),
        [whole] * 8,
        flops=4 * 64 * width * size,
        moved=4 * width * size,
        out_specs=(whole,) * 5,
    )


def update_token(index, size, mine, parts, factor, accum, before):
    rows, tokens = factor.shape
    half = size // 2
    start = index * CHUNK

    def kernel(mine_ref, rx, ry, qy, qx, factor_ref, accum_ref, *rest):
        next_ref, sums_ref = rest[-2:]
        for side, (wide, thin) in enumerate(((rx, ry), (qy, qx))):
            at = side * half
            valid = min(half, tokens - start - at)
            here = slice(start + at, start + at + valid)
            grad = (
                mine_ref[:, at : at + valid]
                + wide[:16, :valid].astype(jnp.float32)
                + thin[:, :valid].astype(jnp.float32)
            )
            total = accum_ref[:, here] + grad * grad
            sums_ref[:, at : at + valid] = total
            next_ref[:, at : at + valid] = factor_ref[:, here] + step_rate * grad * lax.rsqrt(total)

    block = pl.BlockSpec((rows, CHUNK), lambda i: (0, index))
    extra = () if before is None else tuple(before)
    return call(
        kernel,
        (jax.ShapeDtypeStruct(factor.shape, jnp.float32),) * 2,
        (mine, *parts, factor, accum) + extra,
        [whole] * 7 + [pl.BlockSpec(memory_space=pl.ANY)] * len(extra),
        moved=16 * rows * size,
        grid=(1,),
        out_specs=(block, block),
        input_output_aliases={7: 0, 8: 1} if extra else {},
    )


def shards(counts, u_factor, u_accum, v_factor, v_accum):
    tokens = v_factor.shape[1]
    by_token = counts.T
    place = jnp.stack([lax.axis_index("tok"), lax.axis_index("ten")]).astype(jnp.int32)
    ten = lambda a, bit: swap(a, "ten", bit, 4)
    tok = lambda a, bit: swap(a, "tok", bit, 8)

    chunks = []
    for index, start in enumerate(range(0, tokens, CHUNK)):
        size = min(CHUNK, -(-(tokens - start) // (2 * LANES)) * 2 * LANES)
        chunks.append((index, start, size))

    with jax.named_scope("gather_tokens"):
        held = []
        for index, start, size in chunks:
            own = v_factor[:, start : start + size].astype(jnp.bfloat16)
            own = jnp.pad(own, ((0, 0), (0, size - own.shape[1])))
            x, y = ten(own, 1), ten(own, 2)
            held.append((own, x, y, ten(x[:, : size // 2], 2), ten(y[:, size // 2 :], 1)))

    with jax.named_scope("gather_tenants"):
        stack = jnp.concatenate([u_factor, u_accum], axis=0)[None]
        for bit in (1, 2, 4):
            stack = jnp.concatenate([stack, tok(stack, bit)], axis=0)
        factor, accum, half_low = order_tenant(place, stack)

    with jax.named_scope("tenant_grad"):
        grad = None
        for (index, start, size), blocks in zip(chunks, held):
            grad = tenant_grad(start, size, half_low, blocks, by_token, grad)
        for bit in (1, 2):
            grad = grad + tok(grad, bit)
        low, half_low, u_next, u_accum_next = update_tenant(place, grad, tok(grad, 4), factor, accum)

    with jax.named_scope("token_grad"):
        outs = None
        for (index, start, size), blocks in reversed(list(zip(chunks, held))):
            mine, sx, kx, sy, ky = token_grad(start, size, low, half_low, blocks, by_token)
            rx, qy = ten(sx, 1), ten(sy, 2)
            ry = ten((kx + rx[16:].astype(jnp.float32)).astype(jnp.bfloat16), 2)
            qx = ten((ky + qy[16:].astype(jnp.float32)).astype(jnp.bfloat16), 1)
            outs = update_token(index, size, mine, (rx, ry, qy, qx), v_factor, v_accum, outs)
    return (u_next, u_accum_next, *outs)


def solution(mesh):
    def program(counts, u_factor, u_accum, v_factor, v_accum):
        rank, tenants = u_factor.shape
        tokens = v_factor.shape[1] // mesh.shape["tok"]
        suits = (
            mesh.shape["ten"] == 4
            and mesh.shape["tok"] == 8
            and rank == 64
            and tenants == 4 * 256
            and tokens % 16 == 0
        )
        return jax.shard_map(
            shards if suits else shards_any,
            mesh=mesh,
            in_specs=(
                P("ten", "tok"),
                P("tok", "ten"),
                P("tok", "ten"),
                P("ten", "tok"),
                P("ten", "tok"),
            ),
            out_specs=(P("tok", "ten"), P("tok", "ten"), P("ten", "tok"), P("ten", "tok")),
            check_vma=False,
        )(counts, u_factor, u_accum, v_factor, v_accum)

    return program
```

```python
import jax
import jax.numpy as jnp
from jax import lax
from jax.experimental import pallas as pl
from jax.experimental.pallas import tpu as pltpu
from jax.sharding import PartitionSpec as P

weight_scale = 0.5
step_rate = 0.3
LANES = 128
CHUNK = 5376
INNER = 1024
PASS_COST = 64
HBM_SIDE_LIMIT = 34 * 2**20
VMEM_LIMIT = 12 * 2**20

whole = pl.BlockSpec(memory_space=pltpu.VMEM)
scalars = pl.BlockSpec(memory_space=pltpu.SMEM)


def residual(low_tile, v_tile, counts):
    logits = lax.dot_general(
        low_tile, v_tile, (((0,), (0,)), ((), ())), preferred_element_type=jnp.float32
    )
    weighted = weight_scale * counts.astype(jnp.float32)
    return (weighted - (1.0 + weighted) * jax.nn.sigmoid(logits)).astype(jnp.bfloat16)


def gather_tenant(low_rows):
    return lax.all_gather(low_rows, "tok", axis=0, tiled=True)


def shards_any(counts, u_factor, u_accum, v_factor, v_accum):
    v_tile = lax.all_gather(v_factor.astype(jnp.bfloat16), "ten", axis=0, tiled=True)
    u_tile = gather_tenant(u_factor.astype(jnp.bfloat16))
    resid = residual(u_tile, v_tile, counts)
    grad_u = lax.psum_scatter(
        lax.dot_general(
            v_tile, resid, (((1,), (1,)), ((), ())), preferred_element_type=jnp.float32
        ),
        "tok",
        scatter_dimension=0,
        tiled=True,
    )
    u_accum_next = u_accum + grad_u * grad_u
    u_next = u_factor + step_rate * grad_u / jnp.sqrt(u_accum_next)
    u_fresh = gather_tenant(u_next.astype(jnp.bfloat16))
    resid_fresh = residual(u_fresh, v_tile, counts)
    grad_v = lax.psum_scatter(
        jnp.dot(u_fresh, resid_fresh, preferred_element_type=jnp.float32),
        "ten",
        scatter_dimension=0,
        tiled=True,
    )
    v_accum_next = v_accum + grad_v * grad_v
    v_next = v_factor + step_rate * grad_v / jnp.sqrt(v_accum_next)
    return (u_next, u_accum_next, v_next, v_accum_next)


def swap(a, axis, bit, size):
    return lax.ppermute(a, axis, [(i, i ^ bit) for i in range(size)])


def call(kernel, out_shape, operands, in_specs, moved=0, limit=VMEM_LIMIT, **options):
    return pl.pallas_call(
        kernel,
        out_shape=out_shape,
        in_specs=in_specs,
        compiler_params=pltpu.CompilerParams(vmem_limit_bytes=limit),
        cost_estimate=pl.CostEstimate(
            flops=0, bytes_accessed=moved, transcendentals=0
        ),
        **options,
    )(*operands)


def order_tenant(place, gathered):
    def kernel(place_ref, all_ref, factor_ref, accum_ref, half_ref):
        for j in range(4):
            for h in range(2):
                source = (2 * (place_ref[1] ^ j) + h) ^ place_ref[0]
                rows = pl.ds(16 * j + 8 * h, 8)
                factor_ref[rows, :] = all_ref[source, :8, :]
                accum_ref[rows, :] = all_ref[source, 8:, :]
        half_ref[...] = (factor_ref[...].astype(jnp.bfloat16).astype(jnp.float32) * 0.5).astype(
            jnp.bfloat16
        )

    width = gathered.shape[2]
    return call(
        kernel,
        (
            jax.ShapeDtypeStruct((64, width), jnp.float32),
            jax.ShapeDtypeStruct((64, width), jnp.float32),
            jax.ShapeDtypeStruct((64, width), jnp.bfloat16),
        ),
        (place, gathered),
        [scalars, whole],
        out_specs=(whole, whole, whole),
    )


def pieces(start, size, cuts, tokens):
    found, at = [], start
    while at < start + size:
        stop = min([start + size, at + INNER] + [cut for cut in cuts if cut > at])
        found.append((at, stop - at, max(0, min(stop, tokens) - at)))
        at = stop
    return found


def stage(counts, after):
    tokens, width = counts.shape
    step = -(-tokens // 32) * 8

    def kernel(counts_ref, after_ref, out_ref, sems):
        copies = []
        for i, at in enumerate(range(0, tokens, step)):
            rows = pl.ds(at, min(step, tokens - at))
            copies.append(pltpu.make_async_copy(counts_ref.at[rows, :], out_ref.at[rows, :], sems.at[i]))
        for copy in copies:
            copy.start()
        for copy in copies:
            copy.wait()

    return call(
        kernel,
        jax.ShapeDtypeStruct((tokens, width), jnp.int32),
        (counts, after),
        [pl.BlockSpec(memory_space=pltpu.HBM)] * 2,
        moved=8 * tokens * width,
        limit=HBM_SIDE_LIMIT,
        out_specs=whole,
        scratch_shapes=[pltpu.SemaphoreType.DMA((4,))],
    )


def lifted(part):
    return part.astype(jnp.float32) * 0.25 + 0.5


def fresh_residual(half_low, v, lift):
    valid = lift.shape[0]
    logits = lax.dot_general(
        v, half_low, (((0,), (0,)), ((), ())), preferred_element_type=jnp.float32
    )[:valid]
    bend = jnp.tanh(logits)
    resid = (lift - lift * bend - 1.0).astype(jnp.bfloat16)
    if valid < v.shape[1]:
        pad = jnp.zeros((v.shape[1] - valid, resid.shape[1]), jnp.bfloat16)
        resid = jnp.concatenate([resid, pad], axis=0)
    return resid


def gathered(blocks, at, length):
    own, x, y, d0, d1 = blocks
    middle = d0.shape[1]
    diag = d0[:, at : at + length] if at < middle else d1[:, at - middle : at - middle + length]
    return jnp.concatenate([r[:, at : at + length] for r in (own, x, y)] + [diag], axis=0)


def tenant_grad(half_low, blocks, counts):
    tokens, width = counts.shape
    padded = blocks[0].shape[1]

    def kernel(half_ref, *refs):
        blocks_ref, counts_ref, out_ref = refs[:5], refs[5], refs[6]
        grad = jnp.zeros(out_ref.shape, jnp.float32)
        for at, length, valid in pieces(0, padded, [padded // 2], tokens):
            v = gathered(blocks_ref, at, length)
            resid = fresh_residual(half_ref[...], v, lifted(counts_ref[at : at + valid, :]))
            grad += jnp.dot(v, resid, preferred_element_type=jnp.float32)
        out_ref[...] = grad

    return call(
        kernel,
        jax.ShapeDtypeStruct((64, width), jnp.float32),
        (half_low, *blocks, counts),
        [whole] * 7,
        moved=PASS_COST * padded,
        out_specs=whole,
    )


def token_grad(start, size, low, step, blocks, counts):
    tokens, width = counts.shape
    half = size // 2
    ahead = len(step) if step else 2

    def kernel(*refs):
        blocks_ref, counts_ref = refs[ahead : ahead + 5], refs[ahead + 5]
        mine, sx, kx, sy, ky = refs[ahead + 6 : ahead + 11]
        if step:
            place_ref, a_ref, b_ref, factor_ref, accum_ref = refs[:ahead]
            low_ref, half_ref, next_ref, sums_ref, full_ref, total_ref = refs[ahead + 11 :]
            grad = a_ref[...].astype(jnp.float32) + b_ref[...].astype(jnp.float32)
            total = accum_ref[...] + grad * grad
            fresh = factor_ref[...] + step_rate * grad * lax.rsqrt(total)
            full_ref[...] = fresh
            total_ref[...] = total
            low_u = fresh.astype(jnp.bfloat16)
            half_u = (low_u.astype(jnp.float32) * 0.5).astype(jnp.bfloat16)
            low_ref[...] = low_u
            half_ref[...] = half_u
            row = ((place_ref[0] // 2) ^ place_ref[1]) * 16 + (place_ref[0] % 2) * 8
            mine_rows = pl.ds(pl.multiple_of(row, 8), 8)
            next_ref[...] = full_ref[mine_rows, :]
            sums_ref[...] = total_ref[mine_rows, :]
        else:
            low_u, half_u = refs[0][...], refs[1][...]
        middle = start + half
        for at, length, valid in pieces(start, size, [middle, blocks[0].shape[1] // 2], tokens):
            v = gathered(blocks_ref, at, length)
            resid = fresh_residual(half_u, v, lifted(counts_ref[at : at + valid, :]))
            grad = lax.dot_general(
                low_u, resid, (((1,), (1,)), ((), ())), preferred_element_type=jnp.float32
            )
            mine[:, at - start : at - start + length] = grad[:16]
            side = int(at >= middle)
            send, keep = ((sx, kx), (sy, ky))[side]
            first, kept = ((16, 32), (32, 16))[side]
            lo = at - (start, middle)[side]
            here = slice(lo, lo + length)
            send[:16, here] = grad[first : first + 16].astype(jnp.bfloat16)
            send[16:, here] = grad[48:].astype(jnp.bfloat16)
            keep[:, here] = grad[kept : kept + 16]

    shapes = [
        jax.ShapeDtypeStruct((16, size), jnp.float32),
        jax.ShapeDtypeStruct((32, half), jnp.bfloat16),
        jax.ShapeDtypeStruct((16, half), jnp.float32),
        jax.ShapeDtypeStruct((32, half), jnp.bfloat16),
        jax.ShapeDtypeStruct((16, half), jnp.float32),
    ]
    scratch = []
    if step:
        shapes += [jax.ShapeDtypeStruct((64, width), jnp.bfloat16)] * 2
        shapes += [jax.ShapeDtypeStruct((8, width), jnp.float32)] * 2
        scratch = [pltpu.VMEM((64, width), jnp.float32)] * 2
    front = tuple(step) if step else tuple(low)
    return call(
        kernel,
        tuple(shapes),
        front + (*blocks, counts),
        ([scalars] + [whole] * 10) if step else [whole] * 8,
        moved=PASS_COST * size,
        out_specs=(whole,) * len(shapes),
        scratch_shapes=scratch,
    )


def update_token(index, size, mine, parts, factor, accum, before):
    rows, tokens = factor.shape
    half = size // 2
    start = index * CHUNK

    def kernel(mine_ref, rx, ry, qy, qx, factor_ref, accum_ref, *rest):
        next_ref, sums_ref = rest[-2:]
        for side, (wide, thin) in enumerate(((rx, ry), (qy, qx))):
            at = side * half
            valid = min(half, tokens - start - at)
            here = slice(start + at, start + at + valid)
            grad = (
                mine_ref[:, at : at + valid]
                + wide[:16, :valid].astype(jnp.float32)
                + thin[:, :valid].astype(jnp.float32)
            )
            total = accum_ref[:, here] + grad * grad
            sums_ref[:, at : at + valid] = total
            next_ref[:, at : at + valid] = factor_ref[:, here] + step_rate * grad * lax.rsqrt(total)

    block = pl.BlockSpec((rows, CHUNK), lambda i: (0, index))
    extra = () if before is None else tuple(before)
    return call(
        kernel,
        (jax.ShapeDtypeStruct(factor.shape, jnp.float32),) * 2,
        (mine, *parts, factor, accum) + extra,
        [whole] * 7 + [pl.BlockSpec(memory_space=pl.ANY)] * len(extra),
        moved=16 * rows * size,
        grid=(1,),
        out_specs=(block, block),
        input_output_aliases={7: 0, 8: 1} if extra else {},
    )


def shards(counts, u_factor, u_accum, v_factor, v_accum):
    tokens = v_factor.shape[1]
    by_token = counts.T
    place = jnp.stack([lax.axis_index("tok"), lax.axis_index("ten")]).astype(jnp.int32)
    ten = lambda a, bit: swap(a, "ten", bit, 4)
    tok = lambda a, bit: swap(a, "tok", bit, 8)

    padded = -(-tokens // (2 * LANES)) * 2 * LANES
    chunks = [(i, s, min(CHUNK, padded - s)) for i, s in enumerate(range(0, padded, CHUNK))]

    with jax.named_scope("gather_tokens"):
        own = jnp.pad(v_factor.astype(jnp.bfloat16), ((0, 0), (0, padded - tokens)))
        x, y = ten(own, 1), ten(own, 2)
        d0, d1 = x[:, : padded // 2], y[:, padded // 2 :]
        relayed = (d0, d1)
        blocks = (own, x, y, ten(d0, 2), ten(d1, 1))

    with jax.named_scope("gather_tenants"):
        stack = jnp.concatenate([u_factor, u_accum], axis=0)[None]
        for bit in (1, 2, 4):
            stack = jnp.concatenate([stack, tok(stack, bit)], axis=0)
            if bit == 1:
                staged = stage(by_token, stack)
            elif bit == 2:
                stack, staged, _, _ = lax.optimization_barrier((stack, staged, *relayed))
        factor, accum, half_low = order_tenant(place, stack)

    with jax.named_scope("tenant_grad"):
        grad = tenant_grad(half_low, blocks, staged)
        grad = (grad + tok(grad, 1)).astype(jnp.bfloat16)
        grad = grad.astype(jnp.float32) + tok(grad, 2).astype(jnp.float32)
        grad = grad.astype(jnp.bfloat16)

    with jax.named_scope("token_grad"):
        outs, ahead, low, step = None, None, None, (place, grad, tok(grad, 4), factor, accum)
        for index, start, size in chunks:
            made = token_grad(start, size, low, step, blocks, staged)
            mine, sx, kx, sy, ky = made[:5]
            if step:
                low, u_next, u_accum_next, step = made[5:7], made[7], made[8], None
            rx, qy = ten(sx, 1), ten(sy, 2)
            if ahead is not None:
                kx, ky, _, _ = lax.optimization_barrier((kx, ky, *ahead))
            ahead = (
                (kx + rx[16:].astype(jnp.float32)).astype(jnp.bfloat16),
                (ky + qy[16:].astype(jnp.float32)).astype(jnp.bfloat16),
            )
            ry, qx = ten(ahead[0], 2), ten(ahead[1], 1)
            outs = update_token(index, size, mine, (rx, ry, qy, qx), v_factor, v_accum, outs)
    return (u_next, u_accum_next, *outs)


def solution(mesh):
    def program(counts, u_factor, u_accum, v_factor, v_accum):
        rank, tenants = u_factor.shape
        tokens = v_factor.shape[1] // mesh.shape["tok"]
        suits = (
            mesh.shape["ten"] == 4
            and mesh.shape["tok"] == 8
            and rank == 64
            and tenants == 4 * 256
            and tokens % 16 == 0
            and CHUNK < tokens
        )
        return jax.shard_map(
            shards if suits else shards_any,
            mesh=mesh,
            in_specs=(
                P("ten", "tok"),
                P("tok", "ten"),
                P("tok", "ten"),
                P("ten", "tok"),
                P("ten", "tok"),
            ),
            out_specs=(P("tok", "ten"), P("tok", "ten"), P("ten", "tok"), P("ten", "tok")),
            check_vma=False,
        )(counts, u_factor, u_accum, v_factor, v_accum)

    return program
```

```python
import jax
import jax.numpy as jnp
from jax import lax
from jax.experimental import pallas as pl
from jax.experimental.pallas import tpu as pltpu
from jax.sharding import PartitionSpec as P

weight_scale = 0.5
step_rate = 0.3
LANES = 128
CHUNKS = (5376, 5376)
GROUP = sum(CHUNKS)
INNER = 1024
PASS_COST = 64
HBM_SIDE_LIMIT = 34 * 2**20
VMEM_LIMIT = 12 * 2**20

whole = pl.BlockSpec(memory_space=pltpu.VMEM)
scalars = pl.BlockSpec(memory_space=pltpu.SMEM)


def residual(low_tile, v_tile, counts):
    logits = lax.dot_general(
        low_tile, v_tile, (((0,), (0,)), ((), ())), preferred_element_type=jnp.float32
    )
    weighted = weight_scale * counts.astype(jnp.float32)
    return (weighted - (1.0 + weighted) * jax.nn.sigmoid(logits)).astype(jnp.bfloat16)


def gather_tenant(low_rows):
    return lax.all_gather(low_rows, "tok", axis=0, tiled=True)


def shards_any(counts, u_factor, u_accum, v_factor, v_accum):
    v_tile = lax.all_gather(v_factor.astype(jnp.bfloat16), "ten", axis=0, tiled=True)
    u_tile = gather_tenant(u_factor.astype(jnp.bfloat16))
    resid = residual(u_tile, v_tile, counts)
    grad_u = lax.psum_scatter(
        lax.dot_general(
            v_tile, resid, (((1,), (1,)), ((), ())), preferred_element_type=jnp.float32
        ),
        "tok",
        scatter_dimension=0,
        tiled=True,
    )
    u_accum_next = u_accum + grad_u * grad_u
    u_next = u_factor + step_rate * grad_u / jnp.sqrt(u_accum_next)
    u_fresh = gather_tenant(u_next.astype(jnp.bfloat16))
    resid_fresh = residual(u_fresh, v_tile, counts)
    grad_v = lax.psum_scatter(
        jnp.dot(u_fresh, resid_fresh, preferred_element_type=jnp.float32),
        "ten",
        scatter_dimension=0,
        tiled=True,
    )
    v_accum_next = v_accum + grad_v * grad_v
    v_next = v_factor + step_rate * grad_v / jnp.sqrt(v_accum_next)
    return (u_next, u_accum_next, v_next, v_accum_next)


def swap(a, axis, bit, size):
    return lax.ppermute(a, axis, [(i, i ^ bit) for i in range(size)])


def call(kernel, out_shape, operands, in_specs, moved=0, limit=VMEM_LIMIT, **options):
    return pl.pallas_call(
        kernel,
        out_shape=out_shape,
        in_specs=in_specs,
        compiler_params=pltpu.CompilerParams(vmem_limit_bytes=limit),
        cost_estimate=pl.CostEstimate(
            flops=0, bytes_accessed=moved, transcendentals=0
        ),
        **options,
    )(*operands)


def order_tenant(place, gathered):
    def kernel(place_ref, all_ref, factor_ref, accum_ref, half_ref):
        for j in range(4):
            for h in range(2):
                source = (2 * (place_ref[1] ^ j) + h) ^ place_ref[0]
                rows = pl.ds(16 * j + 8 * h, 8)
                factor_ref[rows, :] = all_ref[source, :8, :]
                accum_ref[rows, :] = all_ref[source, 8:, :]
        half_ref[...] = (factor_ref[...].astype(jnp.bfloat16).astype(jnp.float32) * 0.5).astype(
            jnp.bfloat16
        )

    width = gathered.shape[2]
    return call(
        kernel,
        (
            jax.ShapeDtypeStruct((64, width), jnp.float32),
            jax.ShapeDtypeStruct((64, width), jnp.float32),
            jax.ShapeDtypeStruct((64, width), jnp.bfloat16),
        ),
        (place, gathered),
        [scalars, whole],
        out_specs=(whole, whole, whole),
    )


def pieces(start, size, cuts, tokens):
    found, at = [], start
    while at < start + size:
        stop = min([start + size, at + INNER] + [cut for cut in cuts if cut > at])
        found.append((at, stop - at, max(0, min(stop, tokens) - at)))
        at = stop
    return found


def stage(counts, after):
    tokens, width = counts.shape
    step = -(-tokens // 32) * 8

    def kernel(counts_ref, after_ref, out_ref, sems):
        copies = []
        for i, at in enumerate(range(0, tokens, step)):
            rows = pl.ds(at, min(step, tokens - at))
            copies.append(pltpu.make_async_copy(counts_ref.at[rows, :], out_ref.at[rows, :], sems.at[i]))
        for copy in copies:
            copy.start()
        for copy in copies:
            copy.wait()

    return call(
        kernel,
        jax.ShapeDtypeStruct((tokens, width), jnp.int32),
        (counts, after),
        [pl.BlockSpec(memory_space=pltpu.HBM)] * 2,
        moved=8 * tokens * width,
        limit=HBM_SIDE_LIMIT,
        out_specs=whole,
        scratch_shapes=[pltpu.SemaphoreType.DMA((4,))],
    )


def lifted(part):
    return part.astype(jnp.float32) * 0.25 + 0.5


def fresh_residual(half_low, v, lift):
    valid = lift.shape[0]
    logits = lax.dot_general(
        v, half_low, (((0,), (0,)), ((), ())), preferred_element_type=jnp.float32
    )[:valid]
    bend = jnp.tanh(logits)
    resid = (lift - lift * bend - 1.0).astype(jnp.bfloat16)
    if valid < v.shape[1]:
        pad = jnp.zeros((v.shape[1] - valid, resid.shape[1]), jnp.bfloat16)
        resid = jnp.concatenate([resid, pad], axis=0)
    return resid


def gathered(blocks, at, length):
    own, x, y, d0, d1 = blocks
    middle = d0.shape[1]
    diag = d0[:, at : at + length] if at < middle else d1[:, at - middle : at - middle + length]
    return jnp.concatenate([r[:, at : at + length] for r in (own, x, y)] + [diag], axis=0)


def tenant_grad(half_low, blocks, counts):
    tokens, width = counts.shape
    padded = blocks[0].shape[1]

    def kernel(half_ref, *refs):
        blocks_ref, counts_ref, out_ref = refs[:5], refs[5], refs[6]
        grad = jnp.zeros(out_ref.shape, jnp.float32)
        for at, length, valid in pieces(0, padded, [padded // 2], tokens):
            v = gathered(blocks_ref, at, length)
            resid = fresh_residual(half_ref[...], v, lifted(counts_ref[at : at + valid, :]))
            grad += jnp.dot(v, resid, preferred_element_type=jnp.float32)
        out_ref[...] = grad

    return call(
        kernel,
        jax.ShapeDtypeStruct((64, width), jnp.float32),
        (half_low, *blocks, counts),
        [whole] * 7,
        moved=PASS_COST * padded,
        out_specs=whole,
    )


def token_grad(start, size, low, step, blocks, counts, after):
    tokens, width = counts.shape
    half = size // 2
    ahead = len(step) if step else 2

    def kernel(*refs):
        refs = refs if after is None else refs[1:]
        blocks_ref, counts_ref = refs[ahead : ahead + 5], refs[ahead + 5]
        mine, sx, kx, sy, ky = refs[ahead + 6 : ahead + 11]
        if step:
            a_ref, b_ref, factor_ref, accum_ref = refs[:ahead]
            low_ref, half_ref, next_ref, sums_ref = refs[ahead + 11 :]
            grad = a_ref[...].astype(jnp.float32) + b_ref[...].astype(jnp.float32)
            total = accum_ref[...] + grad * grad
            fresh = factor_ref[...] + step_rate * grad * lax.rsqrt(total)
            next_ref[...] = fresh
            sums_ref[...] = total
            low_u = fresh.astype(jnp.bfloat16)
            half_u = (low_u.astype(jnp.float32) * 0.5).astype(jnp.bfloat16)
            low_ref[...] = low_u
            half_ref[...] = half_u
        else:
            low_u, half_u = refs[0][...], refs[1][...]
        middle = start + half
        for at, length, valid in pieces(start, size, [middle, blocks[0].shape[1] // 2], tokens):
            v = gathered(blocks_ref, at, length)
            resid = fresh_residual(half_u, v, lifted(counts_ref[at : at + valid, :]))
            grad = lax.dot_general(
                low_u, resid, (((1,), (1,)), ((), ())), preferred_element_type=jnp.float32
            )
            mine[:, at - start : at - start + length] = grad[:16]
            side = int(at >= middle)
            send, keep = ((sx, kx), (sy, ky))[side]
            first, kept = ((16, 32), (32, 16))[side]
            lo = at - (start, middle)[side]
            here = slice(lo, lo + length)
            send[:16, here] = grad[first : first + 16].astype(jnp.bfloat16)
            send[16:, here] = grad[48:].astype(jnp.bfloat16)
            keep[:, here] = grad[kept : kept + 16]

    shapes = [
        jax.ShapeDtypeStruct((16, size), jnp.float32),
        jax.ShapeDtypeStruct((32, half), jnp.bfloat16),
        jax.ShapeDtypeStruct((16, half), jnp.float32),
        jax.ShapeDtypeStruct((32, half), jnp.bfloat16),
        jax.ShapeDtypeStruct((16, half), jnp.float32),
    ]
    if step:
        shapes += [jax.ShapeDtypeStruct((64, width), jnp.bfloat16)] * 2
        shapes += [jax.ShapeDtypeStruct((64, width), jnp.float32)] * 2
    front = tuple(step) if step else tuple(low)
    return call(
        kernel,
        tuple(shapes),
        (() if after is None else (after,)) + front + (*blocks, counts),
        [pl.BlockSpec(memory_space=pl.ANY)] * (after is not None) + [whole] * (10 if step else 8),
        moved=PASS_COST * size,
        out_specs=(whole,) * len(shapes),
    )


def update_token(index, group, made, relayed, factor, accum, before, tenant):
    rows, tokens = factor.shape
    parts = [part for one in made for part in one]

    def kernel(*refs):
        chunk_refs, (ry, qx) = refs[: len(parts)], refs[len(parts) : len(parts) + 2]
        factor_ref, accum_ref = refs[len(parts) + 2 : len(parts) + 4]
        outs = refs[len(parts) + 4 + len(extra) :]
        done = 0
        for i, (start, size) in enumerate(group):
            mine_ref, rx, qy = chunk_refs[3 * i : 3 * i + 3]
            half = size // 2
            for side, (wide, thin) in enumerate(((rx, ry), (qy, qx))):
                at = side * half
                valid = min(half, tokens - start - at)
                here = slice(start + at, start + at + valid)
                out = slice(start - group[0][0] + at, start - group[0][0] + at + valid)
                grad = (
                    mine_ref[:, at : at + valid]
                    + wide[:16, :valid].astype(jnp.float32)
                    + thin[:, done : done + valid].astype(jnp.float32)
                )
                total = accum_ref[:, here] + grad * grad
                outs[1][:, out] = total
                outs[0][:, out] = factor_ref[:, here] + step_rate * grad * lax.rsqrt(total)
            done += half
        if tenant is not None:
            place_ref, next_ref, sums_ref = refs[len(parts) + 4 : len(parts) + 7]
            row = ((place_ref[0] // 2) ^ place_ref[1]) * 16 + (place_ref[0] % 2) * 8
            mine_rows = pl.ds(pl.multiple_of(row, 8), 8)
            outs[2][...] = next_ref[mine_rows, :]
            outs[3][...] = sums_ref[mine_rows, :]

    block = pl.BlockSpec((rows, GROUP), lambda i: (0, index))
    shapes, specs = [jax.ShapeDtypeStruct(factor.shape, jnp.float32)] * 2, [block] * 2
    extra, extra_specs = (), []
    if before is not None:
        extra, extra_specs = tuple(before), [pl.BlockSpec(memory_space=pl.ANY)] * 2
    if tenant is not None:
        extra, extra_specs = tuple(tenant), [scalars, whole, whole]
        shapes += [jax.ShapeDtypeStruct((8, tenant[1].shape[1]), jnp.float32)] * 2
        specs += [whole] * 2
    return call(
        kernel,
        tuple(shapes),
        (*parts, *relayed, factor, accum) + extra,
        [whole] * (len(parts) + 4) + extra_specs,
        moved=16 * rows * GROUP,
        grid=(1,),
        out_specs=tuple(specs),
        input_output_aliases={len(parts) + 4: 0, len(parts) + 5: 1} if before is not None else {},
    )


def shards(counts, u_factor, u_accum, v_factor, v_accum):
    tokens = v_factor.shape[1]
    by_token = counts.T
    place = jnp.stack([lax.axis_index("tok"), lax.axis_index("ten")]).astype(jnp.int32)
    ten = lambda a, bit: swap(a, "ten", bit, 4)
    tok = lambda a, bit: swap(a, "tok", bit, 8)

    padded = -(-tokens // (2 * LANES)) * 2 * LANES
    groups = [[(0, CHUNKS[0]), (CHUNKS[0], CHUNKS[1])], [(GROUP, padded - GROUP)]]

    with jax.named_scope("gather_tokens"):
        own = jnp.pad(v_factor.astype(jnp.bfloat16), ((0, 0), (0, padded - tokens)))
        x, y = ten(own, 1), ten(own, 2)
        d0, d1 = x[:, : padded // 2], y[:, padded // 2 :]
        relayed = (d0, d1)
        blocks = (own, x, y, ten(d0, 2), ten(d1, 1))

    with jax.named_scope("gather_tenants"):
        stack = jnp.concatenate([u_factor, u_accum], axis=0)[None]
        for bit in (1, 2, 4):
            stack = jnp.concatenate([stack, tok(stack, bit)], axis=0)
            if bit == 1:
                staged = stage(by_token, stack)
            elif bit == 2:
                stack, staged, _, _ = lax.optimization_barrier((stack, staged, *relayed))
        factor, accum, half_low = order_tenant(place, stack)

    with jax.named_scope("tenant_grad"):
        grad = tenant_grad(half_low, blocks, staged)
        grad = (grad + tok(grad, 1)).astype(jnp.bfloat16)
        grad = grad.astype(jnp.float32) + tok(grad, 2).astype(jnp.float32)
        grad = grad.astype(jnp.bfloat16)

    with jax.named_scope("token_grad"):
        outs, ahead, after, low, step = None, None, None, None, (grad, tok(grad, 4), factor, accum)
        for index, group in enumerate(groups):
            made, add_x, add_y = [], [], []
            for start, size in group:
                mine, sx, kx, sy, ky, *news = token_grad(start, size, low, step, blocks, staged, after)
                after = ky
                if step:
                    low, tenant, step = news[:2], (place, *news[2:]), None
                rx, qy = ten(sx, 1), ten(sy, 2)
                if ahead is not None:
                    kx, ky, _, _ = lax.optimization_barrier((kx, ky, *ahead))
                made.append((mine, rx, qy))
                add_x.append((kx + rx[16:].astype(jnp.float32)).astype(jnp.bfloat16))
                add_y.append((ky + qy[16:].astype(jnp.float32)).astype(jnp.bfloat16))
            ahead = (jnp.concatenate(add_x, axis=1), jnp.concatenate(add_y, axis=1))
            relayed = (ten(ahead[0], 2), ten(ahead[1], 1))
            outs = update_token(index, group, made, relayed, v_factor, v_accum, outs, tenant)
            if tenant is not None:
                u_next, u_accum_next, tenant = outs[2], outs[3], None
            outs = outs[:2]
    return (u_next, u_accum_next, *outs)


def solution(mesh):
    def program(counts, u_factor, u_accum, v_factor, v_accum):
        rank, tenants = u_factor.shape
        tokens = v_factor.shape[1] // mesh.shape["tok"]
        suits = (
            mesh.shape["ten"] == 4
            and mesh.shape["tok"] == 8
            and rank == 64
            and tenants == 4 * 256
            and tokens % 16 == 0
            and GROUP < tokens <= 2 * GROUP
        )
        return jax.shard_map(
            shards if suits else shards_any,
            mesh=mesh,
            in_specs=(
                P("ten", "tok"),
                P("tok", "ten"),
                P("tok", "ten"),
                P("ten", "tok"),
                P("ten", "tok"),
            ),
            out_specs=(P("tok", "ten"), P("tok", "ten"), P("ten", "tok"), P("ten", "tok")),
            check_vma=False,
        )(counts, u_factor, u_accum, v_factor, v_accum)

    return program
```

```python
import jax
import jax.numpy as jnp
from jax import lax
from jax.experimental import pallas as pl
from jax.experimental.pallas import tpu as pltpu
from jax.sharding import PartitionSpec as P

weight_scale = 0.5
step_rate = 0.3
LANES = 128
CHUNKS = (5376, 5376)
GROUP = sum(CHUNKS)
INNER = 1024
PASS_COST = 64
HBM_SIDE_LIMIT = 34 * 2**20
VMEM_LIMIT = 12 * 2**20

whole = pl.BlockSpec(memory_space=pltpu.VMEM)
scalars = pl.BlockSpec(memory_space=pltpu.SMEM)


def residual(low_tile, v_tile, counts):
    logits = lax.dot_general(
        low_tile, v_tile, (((0,), (0,)), ((), ())), preferred_element_type=jnp.float32
    )
    weighted = weight_scale * counts.astype(jnp.float32)
    return (weighted - (1.0 + weighted) * jax.nn.sigmoid(logits)).astype(jnp.bfloat16)


def gather_tenant(low_rows):
    return lax.all_gather(low_rows, "tok", axis=0, tiled=True)


def shards_any(counts, u_factor, u_accum, v_factor, v_accum):
    v_tile = lax.all_gather(v_factor.astype(jnp.bfloat16), "ten", axis=0, tiled=True)
    u_tile = gather_tenant(u_factor.astype(jnp.bfloat16))
    resid = residual(u_tile, v_tile, counts)
    grad_u = lax.psum_scatter(
        lax.dot_general(
            v_tile, resid, (((1,), (1,)), ((), ())), preferred_element_type=jnp.float32
        ),
        "tok",
        scatter_dimension=0,
        tiled=True,
    )
    u_accum_next = u_accum + grad_u * grad_u
    u_next = u_factor + step_rate * grad_u / jnp.sqrt(u_accum_next)
    u_fresh = gather_tenant(u_next.astype(jnp.bfloat16))
    resid_fresh = residual(u_fresh, v_tile, counts)
    grad_v = lax.psum_scatter(
        jnp.dot(u_fresh, resid_fresh, preferred_element_type=jnp.float32),
        "ten",
        scatter_dimension=0,
        tiled=True,
    )
    v_accum_next = v_accum + grad_v * grad_v
    v_next = v_factor + step_rate * grad_v / jnp.sqrt(v_accum_next)
    return (u_next, u_accum_next, v_next, v_accum_next)


def swap(a, axis, bit, size):
    return lax.ppermute(a, axis, [(i, i ^ bit) for i in range(size)])


def call(kernel, out_shape, operands, in_specs, moved=0, limit=VMEM_LIMIT, **options):
    return pl.pallas_call(
        kernel,
        out_shape=out_shape,
        in_specs=in_specs,
        compiler_params=pltpu.CompilerParams(vmem_limit_bytes=limit),
        cost_estimate=pl.CostEstimate(
            flops=0, bytes_accessed=moved, transcendentals=0
        ),
        **options,
    )(*operands)


def order_tenant(turn, stack):
    def kernel(turn_ref, stack_ref, factor_ref, accum_ref, half_ref):
        for rows, out_ref in ((slice(0, 8), factor_ref), (slice(8, 16), accum_ref)):
            blocks = [stack_ref[p, rows, :] for p in range(8)]
            for bit in (1, 2, 4):
                stays = (turn_ref[...] & bit) == 0
                blocks = [jnp.where(stays, blocks[p], blocks[p ^ bit]) for p in range(8)]
            for p in range(8):
                out_ref[8 * p : 8 * p + 8, :] = blocks[p]
        low = factor_ref[...].astype(jnp.bfloat16).astype(jnp.float32)
        half_ref[...] = (low * 0.5).astype(jnp.bfloat16)

    width = stack.shape[2]
    return call(
        kernel,
        (
            jax.ShapeDtypeStruct((64, width), jnp.float32),
            jax.ShapeDtypeStruct((64, width), jnp.float32),
            jax.ShapeDtypeStruct((64, width), jnp.bfloat16),
        ),
        (turn, stack),
        [whole] * 2,
        out_specs=(whole,) * 3,
    )


def pieces(start, size, cuts, tokens):
    found, at = [], start
    while at < start + size:
        stop = min([start + size, at + INNER] + [cut for cut in cuts if cut > at])
        found.append((at, stop - at, max(0, min(stop, tokens) - at)))
        at = stop
    return found


def stage(turn, counts, after):
    tokens, width = counts.shape
    step = -(-tokens // 32) * 8

    def kernel(turn_ref, counts_ref, after_ref, out_ref, vector_ref, sems):
        copies = []
        for i, at in enumerate(range(0, tokens, step)):
            rows = pl.ds(at, min(step, tokens - at))
            copies.append(pltpu.make_async_copy(counts_ref.at[rows, :], out_ref.at[rows, :], sems.at[i]))
        for copy in copies:
            copy.start()
        vector_ref[...] = jnp.broadcast_to(turn_ref[0], vector_ref.shape)
        for copy in copies:
            copy.wait()

    return call(
        kernel,
        (
            jax.ShapeDtypeStruct((tokens, width), jnp.int32),
            jax.ShapeDtypeStruct((8, width), jnp.int32),
        ),
        (turn, counts, after),
        [scalars] + [pl.BlockSpec(memory_space=pltpu.HBM)] * 2,
        moved=8 * tokens * width,
        limit=HBM_SIDE_LIMIT,
        out_specs=(whole, whole),
        scratch_shapes=[pltpu.SemaphoreType.DMA((4,))],
    )


def lifted(part):
    return part.astype(jnp.float32) * 0.25 + 0.5


def fresh_residual(half_low, v, lift):
    valid = lift.shape[0]
    logits = lax.dot_general(
        v, half_low, (((0,), (0,)), ((), ())), preferred_element_type=jnp.float32
    )[:valid]
    bend = jnp.tanh(logits)
    resid = (lift - lift * bend - 1.0).astype(jnp.bfloat16)
    if valid < v.shape[1]:
        pad = jnp.zeros((v.shape[1] - valid, resid.shape[1]), jnp.bfloat16)
        resid = jnp.concatenate([resid, pad], axis=0)
    return resid


def gathered(blocks, at, length):
    own, x, y, d0, d1 = blocks
    middle = d0.shape[1]
    diag = d0[:, at : at + length] if at < middle else d1[:, at - middle : at - middle + length]
    return jnp.concatenate([r[:, at : at + length] for r in (own, x, y)] + [diag], axis=0)


def tenant_grad(half_low, blocks, counts):
    tokens, width = counts.shape
    padded = blocks[0].shape[1]

    def kernel(half_ref, *refs):
        blocks_ref, counts_ref, out_ref = refs[:5], refs[5], refs[6]
        grad = jnp.zeros(out_ref.shape, jnp.float32)
        for at, length, valid in pieces(0, padded, [padded // 2], tokens):
            v = gathered(blocks_ref, at, length)
            resid = fresh_residual(half_ref[...], v, lifted(counts_ref[at : at + valid, :]))
            grad += jnp.dot(v, resid, preferred_element_type=jnp.float32)
        out_ref[...] = grad

    return call(
        kernel,
        jax.ShapeDtypeStruct((64, width), jnp.float32),
        (half_low, *blocks, counts),
        [whole] * 7,
        moved=PASS_COST * padded,
        out_specs=whole,
    )


def token_grad(start, size, low, step, blocks, counts, after):
    tokens, width = counts.shape
    half = size // 2
    ahead = len(step) if step else 2

    def kernel(*refs):
        refs = refs if after is None else refs[1:]
        blocks_ref, counts_ref = refs[ahead : ahead + 5], refs[ahead + 5]
        mine, sx, kx, sy, ky = refs[ahead + 6 : ahead + 11]
        if step:
            parts_ref, (factor_ref, accum_ref) = refs[:4], refs[4:6]
            low_ref, half_ref, next_ref, sums_ref = refs[ahead + 11 :]
            grad = sum(part[...].astype(jnp.float32) for part in parts_ref)
            total = accum_ref[...] + grad * grad
            fresh = factor_ref[...] + step_rate * grad * lax.rsqrt(total)
            next_ref[...] = fresh
            sums_ref[...] = total
            low_u = fresh.astype(jnp.bfloat16)
            half_u = (low_u.astype(jnp.float32) * 0.5).astype(jnp.bfloat16)
            low_ref[...] = low_u
            half_ref[...] = half_u
        else:
            low_u, half_u = refs[0][...], refs[1][...]
        middle = start + half
        for at, length, valid in pieces(start, size, [middle, blocks[0].shape[1] // 2], tokens):
            v = gathered(blocks_ref, at, length)
            resid = fresh_residual(half_u, v, lifted(counts_ref[at : at + valid, :]))
            grad = lax.dot_general(
                low_u, resid, (((1,), (1,)), ((), ())), preferred_element_type=jnp.float32
            )
            mine[:, at - start : at - start + length] = grad[:16]
            side = int(at >= middle)
            send, keep = ((sx, kx), (sy, ky))[side]
            first, kept = ((16, 32), (32, 16))[side]
            lo = at - (start, middle)[side]
            here = slice(lo, lo + length)
            send[:16, here] = grad[first : first + 16].astype(jnp.bfloat16)
            send[16:, here] = grad[48:].astype(jnp.bfloat16)
            keep[:, here] = grad[kept : kept + 16]

    shapes = [
        jax.ShapeDtypeStruct((16, size), jnp.float32),
        jax.ShapeDtypeStruct((32, half), jnp.bfloat16),
        jax.ShapeDtypeStruct((16, half), jnp.float32),
        jax.ShapeDtypeStruct((32, half), jnp.bfloat16),
        jax.ShapeDtypeStruct((16, half), jnp.float32),
    ]
    if step:
        shapes += [jax.ShapeDtypeStruct((64, width), jnp.bfloat16)] * 2
        shapes += [jax.ShapeDtypeStruct((64, width), jnp.float32)] * 2
    front = tuple(step) if step else tuple(low)
    return call(
        kernel,
        tuple(shapes),
        (() if after is None else (after,)) + front + (*blocks, counts),
        [pl.BlockSpec(memory_space=pl.ANY)] * (after is not None) + [whole] * (12 if step else 8),
        moved=PASS_COST * size,
        out_specs=(whole,) * len(shapes),
    )


def update_token(index, group, made, relayed, factor, accum, before, tenant):
    rows, tokens = factor.shape
    parts = [part for one in made for part in one]

    def kernel(*refs):
        chunk_refs, (ry, qx) = refs[: len(parts)], refs[len(parts) : len(parts) + 2]
        factor_ref, accum_ref = refs[len(parts) + 2 : len(parts) + 4]
        outs = refs[len(parts) + 4 + len(extra) :]
        done = 0
        for i, (start, size) in enumerate(group):
            mine_ref, rx, qy = chunk_refs[3 * i : 3 * i + 3]
            half = size // 2
            for side, (wide, thin) in enumerate(((rx, ry), (qy, qx))):
                at = side * half
                valid = min(half, tokens - start - at)
                here = slice(start + at, start + at + valid)
                out = slice(start - group[0][0] + at, start - group[0][0] + at + valid)
                grad = (
                    mine_ref[:, at : at + valid]
                    + wide[:16, :valid].astype(jnp.float32)
                    + thin[:, done : done + valid].astype(jnp.float32)
                )
                total = accum_ref[:, here] + grad * grad
                outs[1][:, out] = total
                outs[0][:, out] = factor_ref[:, here] + step_rate * grad * lax.rsqrt(total)
            done += half
        if tenant is not None:
            turn_ref, next_ref, sums_ref = refs[len(parts) + 4 : len(parts) + 7]
            mine_rows = pl.ds(pl.multiple_of(8 * turn_ref[0], 8), 8)
            outs[2][...] = next_ref[mine_rows, :]
            outs[3][...] = sums_ref[mine_rows, :]

    block = pl.BlockSpec((rows, GROUP), lambda i: (0, index))
    shapes, specs = [jax.ShapeDtypeStruct(factor.shape, jnp.float32)] * 2, [block] * 2
    extra, extra_specs = (), []
    if before is not None:
        extra, extra_specs = tuple(before), [pl.BlockSpec(memory_space=pl.ANY)] * 2
    if tenant is not None:
        extra, extra_specs = tuple(tenant), [scalars, whole, whole]
        shapes += [jax.ShapeDtypeStruct((8, tenant[1].shape[1]), jnp.float32)] * 2
        specs += [whole] * 2
    return call(
        kernel,
        tuple(shapes),
        (*parts, *relayed, factor, accum) + extra,
        [whole] * (len(parts) + 4) + extra_specs,
        moved=16 * rows * GROUP,
        grid=(1,),
        out_specs=tuple(specs),
        input_output_aliases={len(parts) + 4: 0, len(parts) + 5: 1} if before is not None else {},
    )


def shards(counts, u_factor, u_accum, v_factor, v_accum):
    tokens = v_factor.shape[1]
    by_token = counts.T
    turn = (lax.axis_index("tok") ^ (2 * lax.axis_index("ten"))).astype(jnp.int32)[None]
    ten = lambda a, bit: swap(a, "ten", bit, 4)
    tok = lambda a, bit: swap(a, "tok", bit, 8)

    padded = -(-tokens // (2 * LANES)) * 2 * LANES
    groups = [[(0, CHUNKS[0]), (CHUNKS[0], CHUNKS[1])], [(GROUP, padded - GROUP)]]

    with jax.named_scope("gather_tokens"):
        own = jnp.pad(v_factor.astype(jnp.bfloat16), ((0, 0), (0, padded - tokens)))
        x, y = ten(own, 1), ten(own, 2)
        d0, d1 = x[:, : padded // 2], y[:, padded // 2 :]
        relayed = (d0, d1)
        blocks = (own, x, y, ten(d0, 2), ten(d1, 1))

    with jax.named_scope("gather_tenants"):
        stack = jnp.concatenate([u_factor, u_accum], axis=0)[None]
        for bit in (1, 2, 4):
            stack = jnp.concatenate([stack, tok(stack, bit)], axis=0)
            if bit == 1:
                staged, vector = stage(turn, by_token, stack)
            elif bit == 2:
                stack, vector, _, _ = lax.optimization_barrier((stack, vector, *relayed))
        factor, accum, half_low = order_tenant(vector, stack)

    with jax.named_scope("tenant_grad"):
        grad = tenant_grad(half_low, blocks, staged)
        grad = (grad + tok(grad, 1)).astype(jnp.bfloat16)

    with jax.named_scope("token_grad"):
        outs, ahead, after, low, step = None, None, None, None, (grad, tok(grad, 2), tok(grad, 4), tok(grad, 6), factor, accum)
        for index, group in enumerate(groups):
            made, add_x, add_y = [], [], []
            for start, size in group:
                mine, sx, kx, sy, ky, *news = token_grad(start, size, low, step, blocks, staged, after)
                after = ky
                if step:
                    low, tenant, step = news[:2], (turn, *news[2:]), None
                rx, qy = ten(sx, 1), ten(sy, 2)
                if ahead is not None:
                    kx, ky, _, _ = lax.optimization_barrier((kx, ky, *ahead))
                made.append((mine, rx, qy))
                add_x.append((kx + rx[16:].astype(jnp.float32)).astype(jnp.bfloat16))
                add_y.append((ky + qy[16:].astype(jnp.float32)).astype(jnp.bfloat16))
            ahead = (jnp.concatenate(add_x, axis=1), jnp.concatenate(add_y, axis=1))
            relayed = (ten(ahead[0], 2), ten(ahead[1], 1))
            outs = update_token(index, group, made, relayed, v_factor, v_accum, outs, tenant)
            if tenant is not None:
                u_next, u_accum_next, tenant = outs[2], outs[3], None
            outs = outs[:2]
    return (u_next, u_accum_next, *outs)


def solution(mesh):
    def program(counts, u_factor, u_accum, v_factor, v_accum):
        rank, tenants = u_factor.shape
        tokens = v_factor.shape[1] // mesh.shape["tok"]
        suits = (
            mesh.shape["ten"] == 4
            and mesh.shape["tok"] == 8
            and rank == 64
            and tenants == 4 * 256
            and tokens % 16 == 0
            and GROUP < tokens <= 2 * GROUP
        )
        return jax.shard_map(
            shards if suits else shards_any,
            mesh=mesh,
            in_specs=(
                P("ten", "tok"),
                P("tok", "ten"),
                P("tok", "ten"),
                P("ten", "tok"),
                P("ten", "tok"),
            ),
            out_specs=(P("tok", "ten"), P("tok", "ten"), P("ten", "tok"), P("ten", "tok")),
            check_vma=False,
        )(counts, u_factor, u_accum, v_factor, v_accum)

    return program
```

```python
import jax
import jax.numpy as jnp
from jax import lax
from jax.experimental import pallas as pl
from jax.experimental.pallas import tpu as pltpu
from jax.sharding import PartitionSpec as P

weight_scale = 0.5
step_rate = 0.3
LANES = 128
CHUNKS = (5376, 5376)
GROUP = sum(CHUNKS)
INNER = 1024
CUT = 8192
PASS_COST = 64
HBM_SIDE_LIMIT = 34 * 2**20
VMEM_LIMIT = 12 * 2**20

whole = pl.BlockSpec(memory_space=pltpu.VMEM)
scalars = pl.BlockSpec(memory_space=pltpu.SMEM)


def residual(low_tile, v_tile, counts):
    logits = lax.dot_general(
        low_tile, v_tile, (((0,), (0,)), ((), ())), preferred_element_type=jnp.float32
    )
    weighted = weight_scale * counts.astype(jnp.float32)
    return (weighted - (1.0 + weighted) * jax.nn.sigmoid(logits)).astype(jnp.bfloat16)


def gather_tenant(low_rows):
    return lax.all_gather(low_rows, "tok", axis=0, tiled=True)


def shards_any(counts, u_factor, u_accum, v_factor, v_accum):
    v_tile = lax.all_gather(v_factor.astype(jnp.bfloat16), "ten", axis=0, tiled=True)
    u_tile = gather_tenant(u_factor.astype(jnp.bfloat16))
    resid = residual(u_tile, v_tile, counts)
    grad_u = lax.psum_scatter(
        lax.dot_general(
            v_tile, resid, (((1,), (1,)), ((), ())), preferred_element_type=jnp.float32
        ),
        "tok",
        scatter_dimension=0,
        tiled=True,
    )
    u_accum_next = u_accum + grad_u * grad_u
    u_next = u_factor + step_rate * grad_u / jnp.sqrt(u_accum_next)
    u_fresh = gather_tenant(u_next.astype(jnp.bfloat16))
    resid_fresh = residual(u_fresh, v_tile, counts)
    grad_v = lax.psum_scatter(
        jnp.dot(u_fresh, resid_fresh, preferred_element_type=jnp.float32),
        "ten",
        scatter_dimension=0,
        tiled=True,
    )
    v_accum_next = v_accum + grad_v * grad_v
    v_next = v_factor + step_rate * grad_v / jnp.sqrt(v_accum_next)
    return (u_next, u_accum_next, v_next, v_accum_next)


def swap(a, axis, bit, size):
    return lax.ppermute(a, axis, [(i, i ^ bit) for i in range(size)])


def call(kernel, out_shape, operands, in_specs, moved=0, limit=VMEM_LIMIT, **options):
    return pl.pallas_call(
        kernel,
        out_shape=out_shape,
        in_specs=in_specs,
        compiler_params=pltpu.CompilerParams(vmem_limit_bytes=limit),
        cost_estimate=pl.CostEstimate(
            flops=0, bytes_accessed=moved, transcendentals=0
        ),
        **options,
    )(*operands)


def order_tenant(turn, stack):
    def kernel(turn_ref, stack_ref, factor_ref, accum_ref, half_ref):
        for rows, out_ref in ((slice(0, 8), factor_ref), (slice(8, 16), accum_ref)):
            blocks = [stack_ref[(p >> 1) | ((p & 1) << 2), rows, :] for p in range(8)]
            for bit in (1, 2, 4):
                stays = (turn_ref[...] & bit) == 0
                blocks = [jnp.where(stays, blocks[p], blocks[p ^ bit]) for p in range(8)]
            for p in range(8):
                out_ref[8 * p : 8 * p + 8, :] = blocks[p]
        low = factor_ref[...].astype(jnp.bfloat16).astype(jnp.float32)
        half_ref[...] = (low * 0.5).astype(jnp.bfloat16)

    width = stack.shape[2]
    return call(
        kernel,
        (
            jax.ShapeDtypeStruct((64, width), jnp.float32),
            jax.ShapeDtypeStruct((64, width), jnp.float32),
            jax.ShapeDtypeStruct((64, width), jnp.bfloat16),
        ),
        (turn, stack),
        [whole] * 2,
        out_specs=(whole,) * 3,
    )


def pieces(start, size, cuts, tokens):
    found, at = [], start
    while at < start + size:
        stop = min([start + size, at + INNER] + [cut for cut in cuts if cut > at])
        found.append((at, stop - at, max(0, min(stop, tokens) - at)))
        at = stop
    return found


def stage(turn, counts, after):
    tokens, width = counts.shape
    step = -(-tokens // 32) * 8

    def kernel(turn_ref, counts_ref, after_ref, out_ref, vector_ref, sems):
        copies = []
        for i, at in enumerate(range(0, tokens, step)):
            rows = pl.ds(at, min(step, tokens - at))
            copies.append(pltpu.make_async_copy(counts_ref.at[rows, :], out_ref.at[rows, :], sems.at[i]))
        for copy in copies:
            copy.start()
        vector_ref[...] = jnp.broadcast_to(turn_ref[0], vector_ref.shape)
        for copy in copies:
            copy.wait()

    return call(
        kernel,
        (
            jax.ShapeDtypeStruct((tokens, width), jnp.int32),
            jax.ShapeDtypeStruct((8, width), jnp.int32),
        ),
        (turn, counts, after),
        [scalars] + [pl.BlockSpec(memory_space=pltpu.HBM)] * 2,
        moved=8 * tokens * width,
        limit=HBM_SIDE_LIMIT,
        out_specs=(whole, whole),
        scratch_shapes=[pltpu.SemaphoreType.DMA((4,))],
    )


def lifted(part):
    return part.astype(jnp.float32) * 0.25 + 0.5


def fresh_residual(half_low, v, lift):
    valid = lift.shape[0]
    logits = lax.dot_general(
        v, half_low, (((0,), (0,)), ((), ())), preferred_element_type=jnp.float32
    )[:valid]
    bend = jnp.tanh(logits)
    resid = (lift - lift * bend - 1.0).astype(jnp.bfloat16)
    if valid < v.shape[1]:
        pad = jnp.zeros((v.shape[1] - valid, resid.shape[1]), jnp.bfloat16)
        resid = jnp.concatenate([resid, pad], axis=0)
    return resid


def gathered(blocks, bounds, at, length):
    own, x, y, *diags = blocks
    which = max(i for i, bound in enumerate(bounds) if bound <= at)
    lo = at - bounds[which]
    return jnp.concatenate(
        [r[:, at : at + length] for r in (own, x, y)] + [diags[which][:, lo : lo + length]], axis=0
    )


def tenant_grad(span, half_low, blocks, bounds, counts, total):
    tokens, width = counts.shape
    start, stop = span
    parts = [i for i, bound in enumerate(bounds) if start <= bound < stop]
    extra = () if total is None else (total,)

    def kernel(half_ref, own, x, y, *refs):
        diags = [None] * len(bounds)
        for i, ref in zip(parts, refs):
            diags[i] = ref
        counts_ref, out_ref = refs[len(parts)], refs[-1]
        grad = refs[len(parts) + 1][...] if extra else jnp.zeros(out_ref.shape, jnp.float32)
        for at, length, valid in pieces(start, stop - start, bounds, tokens):
            v = gathered((own, x, y, *diags), bounds, at, length)
            resid = fresh_residual(half_ref[...], v, lifted(counts_ref[at : at + valid, :]))
            grad += jnp.dot(v, resid, preferred_element_type=jnp.float32)
        out_ref[...] = grad

    operands = (half_low, *blocks[:3], *[blocks[3 + i] for i in parts], counts) + extra
    return call(
        kernel,
        jax.ShapeDtypeStruct((64, width), jnp.float32),
        operands,
        [whole] * len(operands),
        moved=PASS_COST * (stop - start),
        out_specs=whole,
    )


def token_grad(start, size, low, step, blocks, bounds, counts, after):
    tokens, width = counts.shape
    half = size // 2
    ahead = len(step) if step else 2

    def kernel(*refs):
        refs = refs if after is None else refs[1:]
        blocks_ref, counts_ref = refs[ahead : ahead + 5], refs[ahead + 5]
        mine, sx, kx, sy, ky = refs[ahead + 6 : ahead + 11]
        if step:
            parts_ref, (factor_ref, accum_ref) = refs[:4], refs[4:6]
            low_ref, half_ref, next_ref, sums_ref = refs[ahead + 11 :]
            grad = sum(part[...].astype(jnp.float32) for part in parts_ref)
            total = accum_ref[...] + grad * grad
            fresh = factor_ref[...] + step_rate * grad * lax.rsqrt(total)
            next_ref[...] = fresh
            sums_ref[...] = total
            low_u = fresh.astype(jnp.bfloat16)
            half_u = (low_u.astype(jnp.float32) * 0.5).astype(jnp.bfloat16)
            low_ref[...] = low_u
            half_ref[...] = half_u
        else:
            low_u, half_u = refs[0][...], refs[1][...]
        middle = start + half
        for at, length, valid in pieces(start, size, [middle, *bounds], tokens):
            v = gathered(blocks_ref, bounds, at, length)
            resid = fresh_residual(half_u, v, lifted(counts_ref[at : at + valid, :]))
            grad = lax.dot_general(
                low_u, resid, (((1,), (1,)), ((), ())), preferred_element_type=jnp.float32
            )
            mine[:, at - start : at - start + length] = grad[:16]
            side = int(at >= middle)
            send, keep = ((sx, kx), (sy, ky))[side]
            first, kept = ((16, 32), (32, 16))[side]
            lo = at - (start, middle)[side]
            here = slice(lo, lo + length)
            send[:16, here] = grad[first : first + 16].astype(jnp.bfloat16)
            send[16:, here] = grad[48:].astype(jnp.bfloat16)
            keep[:, here] = grad[kept : kept + 16]

    shapes = [
        jax.ShapeDtypeStruct((16, size), jnp.float32),
        jax.ShapeDtypeStruct((32, half), jnp.bfloat16),
        jax.ShapeDtypeStruct((16, half), jnp.float32),
        jax.ShapeDtypeStruct((32, half), jnp.bfloat16),
        jax.ShapeDtypeStruct((16, half), jnp.float32),
    ]
    if step:
        shapes += [jax.ShapeDtypeStruct((64, width), jnp.bfloat16)] * 2
        shapes += [jax.ShapeDtypeStruct((64, width), jnp.float32)] * 2
    front = tuple(step) if step else tuple(low)
    return call(
        kernel,
        tuple(shapes),
        (() if after is None else (after,)) + front + (*blocks, counts),
        [pl.BlockSpec(memory_space=pl.ANY)] * (after is not None) + [whole] * (12 if step else 8),
        moved=PASS_COST * size,
        out_specs=(whole,) * len(shapes),
    )


def update_token(index, group, made, relayed, factor, accum, before, tenant):
    rows, tokens = factor.shape
    parts = [part for one in made for part in one]

    def kernel(*refs):
        chunk_refs, (ry, qx) = refs[: len(parts)], refs[len(parts) : len(parts) + 2]
        factor_ref, accum_ref = refs[len(parts) + 2 : len(parts) + 4]
        outs = refs[len(parts) + 4 + len(extra) :]
        done = 0
        for i, (start, size) in enumerate(group):
            mine_ref, rx, qy = chunk_refs[3 * i : 3 * i + 3]
            half = size // 2
            for side, (wide, thin) in enumerate(((rx, ry), (qy, qx))):
                at = side * half
                valid = min(half, tokens - start - at)
                here = slice(start + at, start + at + valid)
                out = slice(start - group[0][0] + at, start - group[0][0] + at + valid)
                grad = (
                    mine_ref[:, at : at + valid]
                    + wide[:16, :valid].astype(jnp.float32)
                    + thin[:, done : done + valid].astype(jnp.float32)
                )
                total = accum_ref[:, here] + grad * grad
                outs[1][:, out] = total
                outs[0][:, out] = factor_ref[:, here] + step_rate * grad * lax.rsqrt(total)
            done += half
        if tenant is not None:
            turn_ref, next_ref, sums_ref = refs[len(parts) + 4 : len(parts) + 7]
            mine_rows = pl.ds(pl.multiple_of(8 * turn_ref[0], 8), 8)
            outs[2][...] = next_ref[mine_rows, :]
            outs[3][...] = sums_ref[mine_rows, :]

    block = pl.BlockSpec((rows, GROUP), lambda i: (0, index))
    shapes, specs = [jax.ShapeDtypeStruct(factor.shape, jnp.float32)] * 2, [block] * 2
    extra, extra_specs = (), []
    if before is not None:
        extra, extra_specs = tuple(before), [pl.BlockSpec(memory_space=pl.ANY)] * 2
    if tenant is not None:
        extra, extra_specs = tuple(tenant), [scalars, whole, whole]
        shapes += [jax.ShapeDtypeStruct((8, tenant[1].shape[1]), jnp.float32)] * 2
        specs += [whole] * 2
    return call(
        kernel,
        tuple(shapes),
        (*parts, *relayed, factor, accum) + extra,
        [whole] * (len(parts) + 4) + extra_specs,
        moved=16 * rows * GROUP,
        grid=(1,),
        out_specs=tuple(specs),
        input_output_aliases={len(parts) + 4: 0, len(parts) + 5: 1} if before is not None else {},
    )


def shards(counts, u_factor, u_accum, v_factor, v_accum):
    tokens = v_factor.shape[1]
    by_token = counts.T
    turn = (lax.axis_index("tok") ^ (2 * lax.axis_index("ten"))).astype(jnp.int32)[None]
    ten = lambda a, bit: swap(a, "ten", bit, 4)
    tok = lambda a, bit: swap(a, "tok", bit, 8)

    padded = -(-tokens // (2 * LANES)) * 2 * LANES
    groups = [[(0, CHUNKS[0]), (CHUNKS[0], CHUNKS[1])], [(GROUP, padded - GROUP)]]

    with jax.named_scope("gather_tokens"):
        own = jnp.pad(v_factor.astype(jnp.bfloat16), ((0, 0), (0, padded - tokens)))
        x, y = ten(own, 1), ten(own, 2)
        bounds = (0, padded // 2)
        relayed = (x[:, : bounds[1]], y[:, bounds[1] :])

    with jax.named_scope("gather_tenants"):
        stack = jnp.concatenate([u_factor, u_accum], axis=0)[None]
        for bit in (2, 4, 1):
            stack = jnp.concatenate([stack, tok(stack, bit)], axis=0)
            if bit == 2:
                staged, vector = stage(turn, by_token, stack[:1])
                stack, vector = lax.optimization_barrier((stack, vector))
        factor, accum, half_low = order_tenant(vector, stack)

    with jax.named_scope("tenant_grad"):
        blocks = (own, x, y, ten(relayed[0], 2), ten(relayed[1], 1))
        spans = [(0, bounds[1]), (bounds[1], padded)]
        grad = tenant_grad(spans[1], half_low, blocks, bounds, staged, None)
        grad = tenant_grad(spans[1 - 1], half_low, blocks, bounds, staged, grad)
        grad = (grad + tok(grad, 1)).astype(jnp.bfloat16)

    with jax.named_scope("token_grad"):
        outs, ahead, after, low, step = None, None, None, None, (grad, tok(grad, 2), tok(grad, 4), tok(grad, 6), factor, accum)
        for index, group in enumerate(groups):
            made, add_x, add_y = [], [], []
            for start, size in group:
                mine, sx, kx, sy, ky, *news = token_grad(start, size, low, step, blocks, bounds, staged, after)
                after = ky
                if step:
                    low, tenant, step = news[:2], (turn, *news[2:]), None
                rx, qy = ten(sx, 1), ten(sy, 2)
                if ahead is not None:
                    kx, ky, _, _ = lax.optimization_barrier((kx, ky, *ahead))
                made.append((mine, rx, qy))
                add_x.append((kx + rx[16:].astype(jnp.float32)).astype(jnp.bfloat16))
                add_y.append((ky + qy[16:].astype(jnp.float32)).astype(jnp.bfloat16))
            ahead = (jnp.concatenate(add_x, axis=1), jnp.concatenate(add_y, axis=1))
            relayed = (ten(ahead[0], 2), ten(ahead[1], 1))
            outs = update_token(index, group, made, relayed, v_factor, v_accum, outs, tenant)
            if tenant is not None:
                u_next, u_accum_next, tenant = outs[2], outs[3], None
            outs = outs[:2]
    return (u_next, u_accum_next, *outs)


def solution(mesh):
    def program(counts, u_factor, u_accum, v_factor, v_accum):
        rank, tenants = u_factor.shape
        tokens = v_factor.shape[1] // mesh.shape["tok"]
        suits = (
            mesh.shape["ten"] == 4
            and mesh.shape["tok"] == 8
            and rank == 64
            and tenants == 4 * 256
            and tokens % 16 == 0
            and GROUP < tokens <= 2 * GROUP
        )
        return jax.shard_map(
            shards if suits else shards_any,
            mesh=mesh,
            in_specs=(
                P("ten", "tok"),
                P("tok", "ten"),
                P("tok", "ten"),
                P("ten", "tok"),
                P("ten", "tok"),
            ),
            out_specs=(P("tok", "ten"), P("tok", "ten"), P("ten", "tok"), P("ten", "tok")),
            check_vma=False,
        )(counts, u_factor, u_accum, v_factor, v_accum)

    return program
```

```python
import jax
import jax.numpy as jnp
from jax import lax
from jax.experimental import pallas as pl
from jax.experimental.pallas import tpu as pltpu
from jax.sharding import PartitionSpec as P

weight_scale = 0.5
step_rate = 0.3
LANES = 128
CHUNKS = (5376, 5376)
GROUP = sum(CHUNKS)
INNER = 1024
CUT = 8192
PASS_COST = 64
HBM_SIDE_LIMIT = 34 * 2**20
VMEM_LIMIT = 12 * 2**20

whole = pl.BlockSpec(memory_space=pltpu.VMEM)
scalars = pl.BlockSpec(memory_space=pltpu.SMEM)


def residual(low_tile, v_tile, counts):
    logits = lax.dot_general(
        low_tile, v_tile, (((0,), (0,)), ((), ())), preferred_element_type=jnp.float32
    )
    weighted = weight_scale * counts.astype(jnp.float32)
    return (weighted - (1.0 + weighted) * jax.nn.sigmoid(logits)).astype(jnp.bfloat16)


def gather_tenant(low_rows):
    return lax.all_gather(low_rows, "tok", axis=0, tiled=True)


def shards_any(counts, u_factor, u_accum, v_factor, v_accum):
    v_tile = lax.all_gather(v_factor.astype(jnp.bfloat16), "ten", axis=0, tiled=True)
    u_tile = gather_tenant(u_factor.astype(jnp.bfloat16))
    resid = residual(u_tile, v_tile, counts)
    grad_u = lax.psum_scatter(
        lax.dot_general(
            v_tile, resid, (((1,), (1,)), ((), ())), preferred_element_type=jnp.float32
        ),
        "tok",
        scatter_dimension=0,
        tiled=True,
    )
    u_accum_next = u_accum + grad_u * grad_u
    u_next = u_factor + step_rate * grad_u / jnp.sqrt(u_accum_next)
    u_fresh = gather_tenant(u_next.astype(jnp.bfloat16))
    resid_fresh = residual(u_fresh, v_tile, counts)
    grad_v = lax.psum_scatter(
        jnp.dot(u_fresh, resid_fresh, preferred_element_type=jnp.float32),
        "ten",
        scatter_dimension=0,
        tiled=True,
    )
    v_accum_next = v_accum + grad_v * grad_v
    v_next = v_factor + step_rate * grad_v / jnp.sqrt(v_accum_next)
    return (u_next, u_accum_next, v_next, v_accum_next)


def swap(a, axis, bit, size):
    return lax.ppermute(a, axis, [(i, i ^ bit) for i in range(size)])


def call(kernel, out_shape, operands, in_specs, moved=0, limit=VMEM_LIMIT, **options):
    return pl.pallas_call(
        kernel,
        out_shape=out_shape,
        in_specs=in_specs,
        compiler_params=pltpu.CompilerParams(vmem_limit_bytes=limit),
        cost_estimate=pl.CostEstimate(
            flops=0, bytes_accessed=moved, transcendentals=0
        ),
        **options,
    )(*operands)


def order_tenant(turn, stack):
    def kernel(turn_ref, stack_ref, factor_ref, accum_ref, half_ref):
        for rows, out_ref in ((slice(0, 8), factor_ref), (slice(8, 16), accum_ref)):
            blocks = [stack_ref[(p >> 1) | ((p & 1) << 2), rows, :] for p in range(8)]
            for bit in (1, 2, 4):
                stays = (turn_ref[...] & bit) == 0
                blocks = [jnp.where(stays, blocks[p], blocks[p ^ bit]) for p in range(8)]
            for p in range(8):
                out_ref[8 * p : 8 * p + 8, :] = blocks[p]
        low = factor_ref[...].astype(jnp.bfloat16).astype(jnp.float32)
        half_ref[...] = (low * 0.5).astype(jnp.bfloat16)

    width = stack.shape[2]
    return call(
        kernel,
        (
            jax.ShapeDtypeStruct((64, width), jnp.float32),
            jax.ShapeDtypeStruct((64, width), jnp.float32),
            jax.ShapeDtypeStruct((64, width), jnp.bfloat16),
        ),
        (turn, stack),
        [whole] * 2,
        out_specs=(whole,) * 3,
    )


def pieces(start, size, cuts, tokens):
    found, at = [], start
    while at < start + size:
        stop = min([start + size, at + INNER] + [cut for cut in cuts if cut > at])
        found.append((at, stop - at, max(0, min(stop, tokens) - at)))
        at = stop
    return found


def stage(turn, counts, after):
    tokens, width = counts.shape
    step = -(-tokens // 32) * 8

    def kernel(turn_ref, counts_ref, after_ref, out_ref, vector_ref, sems):
        copies = []
        for i, at in enumerate(range(0, tokens, step)):
            rows = pl.ds(at, min(step, tokens - at))
            copies.append(pltpu.make_async_copy(counts_ref.at[rows, :], out_ref.at[rows, :], sems.at[i]))
        for copy in copies:
            copy.start()
        vector_ref[...] = jnp.broadcast_to(turn_ref[0], vector_ref.shape)
        for copy in copies:
            copy.wait()

    return call(
        kernel,
        (
            jax.ShapeDtypeStruct((tokens, width), jnp.int32),
            jax.ShapeDtypeStruct((8, width), jnp.int32),
        ),
        (turn, counts, after),
        [scalars] + [pl.BlockSpec(memory_space=pltpu.HBM)] * 2,
        moved=8 * tokens * width,
        limit=HBM_SIDE_LIMIT,
        out_specs=(whole, whole),
        scratch_shapes=[pltpu.SemaphoreType.DMA((4,))],
    )


def lifted(part):
    return part.astype(jnp.float32) * 0.25 + 0.5


def fresh_residual(half_low, v, lift):
    valid = lift.shape[0]
    logits = lax.dot_general(
        v, half_low, (((0,), (0,)), ((), ())), preferred_element_type=jnp.float32
    )[:valid]
    bend = jnp.tanh(logits)
    resid = (lift - lift * bend - 1.0).astype(jnp.bfloat16)
    if valid < v.shape[1]:
        pad = jnp.zeros((v.shape[1] - valid, resid.shape[1]), jnp.bfloat16)
        resid = jnp.concatenate([resid, pad], axis=0)
    return resid


def gathered(blocks, bounds, at, length):
    own, x, y, *diags = blocks
    which = max(i for i, bound in enumerate(bounds) if bound <= at)
    lo = at - bounds[which]
    return jnp.concatenate(
        [r[:, at : at + length] for r in (own, x, y)] + [diags[which][:, lo : lo + length]], axis=0
    )


def tenant_grad(span, half_low, blocks, bounds, counts, total):
    tokens, width = counts.shape
    start, stop = span
    parts = [i for i, bound in enumerate(bounds) if start <= bound < stop]
    extra = () if total is None else (total,)

    def kernel(half_ref, own, x, y, *refs):
        diags = [None] * len(bounds)
        for i, ref in zip(parts, refs):
            diags[i] = ref
        counts_ref, out_ref = refs[len(parts)], refs[-1]
        grad = refs[len(parts) + 1][...] if extra else jnp.zeros(out_ref.shape, jnp.float32)
        for at, length, valid in pieces(start, stop - start, bounds, tokens):
            v = gathered((own, x, y, *diags), bounds, at, length)
            resid = fresh_residual(half_ref[...], v, lifted(counts_ref[at : at + valid, :]))
            grad += jnp.dot(v, resid, preferred_element_type=jnp.float32)
        out_ref[...] = grad

    operands = (half_low, *blocks[:3], *[blocks[3 + i] for i in parts], counts) + extra
    return call(
        kernel,
        jax.ShapeDtypeStruct((64, width), jnp.float32),
        operands,
        [whole] * len(operands),
        moved=PASS_COST * (stop - start),
        out_specs=whole,
    )


def token_grad(start, size, low, step, blocks, bounds, counts, after):
    tokens, width = counts.shape
    half = size // 2
    ahead = len(step) if step else 2

    def kernel(*refs):
        refs = refs if after is None else refs[1:]
        blocks_ref, counts_ref = refs[ahead : ahead + 5], refs[ahead + 5]
        mine, sx, kx, sy, ky = refs[ahead + 6 : ahead + 11]
        if step:
            parts_ref, (factor_ref, accum_ref) = refs[:4], refs[4:6]
            low_ref, half_ref, next_ref, sums_ref = refs[ahead + 11 :]
            grad = sum(part[...].astype(jnp.float32) for part in parts_ref)
            total = accum_ref[...] + grad * grad
            fresh = factor_ref[...] + step_rate * grad * lax.rsqrt(total)
            next_ref[...] = fresh
            sums_ref[...] = total
            low_u = fresh.astype(jnp.bfloat16)
            half_u = (low_u.astype(jnp.float32) * 0.5).astype(jnp.bfloat16)
            low_ref[...] = low_u
            half_ref[...] = half_u
        else:
            low_u, half_u = refs[0][...], refs[1][...]
        middle = start + half
        for at, length, valid in pieces(start, size, [middle, *bounds], tokens):
            v = gathered(blocks_ref, bounds, at, length)
            resid = fresh_residual(half_u, v, lifted(counts_ref[at : at + valid, :]))
            grad = lax.dot_general(
                low_u, resid, (((1,), (1,)), ((), ())), preferred_element_type=jnp.float32
            )
            mine[:, at - start : at - start + length] = grad[:16]
            side = int(at >= middle)
            send, keep = ((sx, kx), (sy, ky))[side]
            first, kept = ((16, 32), (32, 16))[side]
            lo = at - (start, middle)[side]
            here = slice(lo, lo + length)
            send[:16, here] = grad[first : first + 16].astype(jnp.bfloat16)
            send[16:, here] = grad[48:].astype(jnp.bfloat16)
            keep[:, here] = grad[kept : kept + 16]

    shapes = [
        jax.ShapeDtypeStruct((16, size), jnp.float32),
        jax.ShapeDtypeStruct((32, half), jnp.bfloat16),
        jax.ShapeDtypeStruct((16, half), jnp.float32),
        jax.ShapeDtypeStruct((32, half), jnp.bfloat16),
        jax.ShapeDtypeStruct((16, half), jnp.float32),
    ]
    if step:
        shapes += [jax.ShapeDtypeStruct((64, width), jnp.bfloat16)] * 2
        shapes += [jax.ShapeDtypeStruct((64, width), jnp.float32)] * 2
    front = tuple(step) if step else tuple(low)
    return call(
        kernel,
        tuple(shapes),
        (() if after is None else (after,)) + front + (*blocks, counts),
        [pl.BlockSpec(memory_space=pl.ANY)] * (after is not None) + [whole] * (12 if step else 8),
        moved=PASS_COST * size,
        out_specs=(whole,) * len(shapes),
    )


def update_token(index, group, made, relayed, factor, accum, before, tenant):
    rows, tokens = factor.shape
    parts = [part for one in made for part in one]

    def kernel(*refs):
        chunk_refs, (ry, qx) = refs[: len(parts)], refs[len(parts) : len(parts) + 2]
        factor_ref, accum_ref = refs[len(parts) + 2 : len(parts) + 4]
        outs = refs[len(parts) + 4 + len(extra) :]
        done = 0
        for i, (start, size) in enumerate(group):
            mine_ref, rx, qy = chunk_refs[3 * i : 3 * i + 3]
            half = size // 2
            for side, (wide, thin) in enumerate(((rx, ry), (qy, qx))):
                at = side * half
                valid = min(half, tokens - start - at)
                here = slice(start + at, start + at + valid)
                out = slice(start - group[0][0] + at, start - group[0][0] + at + valid)
                grad = (
                    mine_ref[:, at : at + valid]
                    + wide[:16, :valid].astype(jnp.float32)
                    + thin[:, done : done + valid].astype(jnp.float32)
                )
                total = accum_ref[:, here] + grad * grad
                outs[1][:, out] = total
                outs[0][:, out] = factor_ref[:, here] + step_rate * grad * lax.rsqrt(total)
            done += half
        if tenant is not None:
            turn_ref, next_ref, sums_ref = refs[len(parts) + 4 : len(parts) + 7]
            mine_rows = pl.ds(pl.multiple_of(8 * turn_ref[0], 8), 8)
            outs[2][...] = next_ref[mine_rows, :]
            outs[3][...] = sums_ref[mine_rows, :]

    block = pl.BlockSpec((rows, GROUP), lambda i: (0, index))
    shapes, specs = [jax.ShapeDtypeStruct(factor.shape, jnp.float32)] * 2, [block] * 2
    extra, extra_specs = (), []
    if before is not None:
        extra, extra_specs = tuple(before), [pl.BlockSpec(memory_space=pl.ANY)] * 2
    if tenant is not None:
        extra, extra_specs = tuple(tenant), [scalars, whole, whole]
        shapes += [jax.ShapeDtypeStruct((8, tenant[1].shape[1]), jnp.float32)] * 2
        specs += [whole] * 2
    return call(
        kernel,
        tuple(shapes),
        (*parts, *relayed, factor, accum) + extra,
        [whole] * (len(parts) + 4) + extra_specs,
        moved=16 * rows * GROUP,
        grid=(1,),
        out_specs=tuple(specs),
        input_output_aliases={len(parts) + 4: 0, len(parts) + 5: 1} if before is not None else {},
    )


def shards(counts, u_factor, u_accum, v_factor, v_accum):
    tokens = v_factor.shape[1]
    by_token = counts.T
    turn = (lax.axis_index("tok") ^ (2 * lax.axis_index("ten"))).astype(jnp.int32)[None]
    ten = lambda a, bit: swap(a, "ten", bit, 4)
    tok = lambda a, bit: swap(a, "tok", bit, 8)

    padded = -(-tokens // (2 * LANES)) * 2 * LANES
    groups = [[(0, CHUNKS[0]), (CHUNKS[0], CHUNKS[1])], [(GROUP, padded - GROUP)]]

    with jax.named_scope("gather_tokens"):
        own = jnp.pad(v_factor.astype(jnp.bfloat16), ((0, 0), (0, padded - tokens)))
        x, y = ten(own, 1), ten(own, 2)
        bounds = (0, 8576)
        relayed = (x[:, : bounds[1]], y[:, bounds[1] :])

    with jax.named_scope("gather_tenants"):
        stack = jnp.concatenate([u_factor, u_accum], axis=0)[None]
        for bit in (2, 4, 1):
            stack = jnp.concatenate([stack, tok(stack, bit)], axis=0)
            if bit == 2:
                staged, vector = stage(turn, by_token, stack[:1])
                stack, vector = lax.optimization_barrier((stack, vector))
        factor, accum, half_low = order_tenant(vector, stack)

    with jax.named_scope("tenant_grad"):
        blocks = (own, x, y, ten(relayed[0], 2), ten(relayed[1], 1))
        spans = [(0, bounds[1]), (bounds[1], padded)]
        grad = tenant_grad(spans[1], half_low, blocks, bounds, staged, None)
        grad = tenant_grad(spans[1 - 1], half_low, blocks, bounds, staged, grad)
        grad = (grad + tok(grad, 1)).astype(jnp.bfloat16)

    with jax.named_scope("token_grad"):
        outs, ahead, after, low, step = None, None, None, None, (grad, tok(grad, 2), tok(grad, 4), tok(grad, 6), factor, accum)
        for index, group in enumerate(groups):
            made, add_x, add_y = [], [], []
            for start, size in group:
                mine, sx, kx, sy, ky, *news = token_grad(start, size, low, step, blocks, bounds, staged, after)
                after = ky
                if step:
                    low, tenant, step = news[:2], (turn, *news[2:]), None
                rx, qy = ten(sx, 1), ten(sy, 2)
                if ahead is not None:
                    kx, ky, _, _ = lax.optimization_barrier((kx, ky, *ahead))
                made.append((mine, rx, qy))
                add_x.append((kx + rx[16:].astype(jnp.float32)).astype(jnp.bfloat16))
                add_y.append((ky + qy[16:].astype(jnp.float32)).astype(jnp.bfloat16))
            ahead = (jnp.concatenate(add_x, axis=1), jnp.concatenate(add_y, axis=1))
            relayed = (ten(ahead[0], 2), ten(ahead[1], 1))
            outs = update_token(index, group, made, relayed, v_factor, v_accum, outs, tenant)
            if tenant is not None:
                u_next, u_accum_next, tenant = outs[2], outs[3], None
            outs = outs[:2]
    return (u_next, u_accum_next, *outs)


def solution(mesh):
    def program(counts, u_factor, u_accum, v_factor, v_accum):
        rank, tenants = u_factor.shape
        tokens = v_factor.shape[1] // mesh.shape["tok"]
        suits = (
            mesh.shape["ten"] == 4
            and mesh.shape["tok"] == 8
            and rank == 64
            and tenants == 4 * 256
            and tokens % 16 == 0
            and GROUP < tokens <= 2 * GROUP
        )
        return jax.shard_map(
            shards if suits else shards_any,
            mesh=mesh,
            in_specs=(
                P("ten", "tok"),
                P("tok", "ten"),
                P("tok", "ten"),
                P("ten", "tok"),
                P("ten", "tok"),
            ),
            out_specs=(P("tok", "ten"), P("tok", "ten"), P("ten", "tok"), P("ten", "tok")),
            check_vma=False,
        )(counts, u_factor, u_accum, v_factor, v_accum)

    return program
```
